512 devices in a mesh: grp: 8 (over z), seg: 64 (over y, x, core).
Axes of the slice: x: 4, y: 8, z: 8, core: 2. Of those that a mesh axis runs over, the one named last changes fastest.
Arguments:
- spectra: bfloat16 [16384, 4096], P(('grp', 'seg')), may hold values from -6 to 6
- gap_counts: int32 [16384], P(('grp', 'seg')), may hold values from 0 to 53999
- band_weight: float32 [2048], replicated, may hold values from 0.1 to 1
- pair_list: int32 [524288, 2], P(('grp', 'seg')), may hold values from 0 to 255, as said below
- stack_owner: int32 [524288, 1], P(('grp', 'seg')), may hold values from 0 to 63; in each aligned block of 1024 rows (0 to 1023, 1024 to 2047, ...) at most 24 rows name the same one
- stack_slot: int32 [524288], P(('grp', 'seg')), may hold values from 0 to 31
Outputs:
- stacked: float32 [16384, 256], P(('grp', 'seg'))
The draws below stay inside these ranges and needn't reach their ends.
Inputs may be any that keep to these rules, and one draw needn't show every extreme that they name: `stack_owner`: among the rows of one device, at most 24 pairs name the same owner, a bound that some block reaches of them. `pair_list`: the two stations of a pair differ, and no unordered pair of stations appears twice among the rows of one station group.
All inputs are finite; a program needn't handle non-finite values.
Results may differ from the reference program's by a relative error of at most 0.0057.
Values may be sent and summed in bfloat16 or wider, within the bound.
No kernel may reach another device: no remote copies, remote signals or barrier semaphores. Data moves between devices by JAX's collectives and lax.ppermute only.
A program may use at most 64 MiB of HBM per device.

```python
import math
import jax
import jax.numpy as jnp
import numpy as np
from jax import lax

F = 2048
LAGS = 256
SAMPLES = 72000
S_DEV = 32
PAIRS_DEV = 1024
SLOTS_DEV = 32
CAP = 24
STATIONS = 16384
PAIRS = 524288
N_GRP = 8
N_SEG = 64


def draw_pair_list(key, part):
    key = jax.random.fold_in(key, 11)
    group_size = S_DEV * N_GRP
    offsets = group_size // 2 - 1
    choices_all = group_size * offsets
    wanted = PAIRS_DEV * N_GRP
    group_keys = jax.random.split(key, N_SEG)

    def one_group(group_key):
        picked = jax.random.permutation(group_key, choices_all)[:wanted].astype(jnp.int32)
        station_one = picked % group_size
        station_two = (station_one + picked // group_size + 1) % group_size
        return jnp.stack([station_one, station_two], axis=1)
    pairs = jax.vmap(one_group)(group_keys)
    flips = jax.random.randint(jax.random.fold_in(key, 5), (N_SEG, wanted, 1), 0, 2).astype(jnp.int32)
    pairs = jnp.where(flips == 1, pairs[:, :, ::-1], pairs)
    pairs = pairs.reshape(N_SEG, N_GRP, PAIRS_DEV, 2)
    pairs = jnp.transpose(pairs, (1, 0, 2, 3)).reshape(N_GRP * N_SEG * PAIRS_DEV, 2)
    return pairs.astype(jnp.int32)


def place_ends(array, rng, low, largest):
    longest = array.shape.index(max(array.shape))
    spots = []
    for shift in (0, 1):
        where = [jax.random.randint(jax.random.fold_in(rng, axis), (), 0, length) for axis, length in enumerate(array.shape)]
        where[longest] = (where[longest] + shift) % array.shape[longest]
        spots.append(tuple(where))
    return array.at[spots[0]].set(low).at[spots[1]].set(largest)


def steps_of(key, dims, pieces, smallest, largest):
    gain, own = 1.0, jax.random.fold_in(key, 6)
    for dim, shards_of in pieces:
        heights = jnp.exp(jax.random.uniform(jax.random.fold_in(own, dim), (shards_of,), jnp.float32, smallest / len(pieces), largest / len(pieces)))
        gain = gain * jnp.repeat(heights, dims[dim] // shards_of).reshape([-1 if axis == dim else 1 for axis in range(len(dims))])
    return gain


def deal_out(stream_key, own, number, rows, amount, top, bound, slope):
    order = jax.random.permutation(stream_key, amount)
    heavy_load, common = portions_of(amount, rows * top, bound, slope, True), portions_of(amount, rows * top, bound, slope, False)
    places = jnp.arange(amount)

    def named(sizes, rotation):
        used = int((sizes > 0).sum())
        fixed = max(1, used // 4)
        passed = fixed + (places - fixed + rotation * (used - fixed)) % max(1, amount - fixed)
        return jnp.zeros((amount,), jnp.int32).at[order[jnp.where(places < fixed, places, passed)]].set(jnp.asarray(sizes, jnp.int32))

    sizes = jnp.where(number % 4 == 0, named(heavy_load, number // 4), named(common, number - number // 4 - 1))
    mixed = jax.random.permutation(jax.random.fold_in(own, 3), amount)
    donor, sink = mixed[0:amount // 2 * 2:2], mixed[1:amount // 2 * 2:2]
    slack = jnp.minimum(sizes[donor] - 1, bound - sizes[sink]) // 2
    slack = jnp.where((donor == order[0]) | (sink == order[0]) | (sizes[sink] == 0), 0, jnp.maximum(slack, 0))
    passed = jax.random.randint(jax.random.fold_in(own, 4), (amount // 2,), 0, 1 << 20) % (slack + 1)
    sizes = sizes.at[donor].add(-passed).at[sink].add(passed)
    members = jnp.searchsorted(jnp.cumsum(sizes), jnp.arange(rows * top), side="right").astype(jnp.int32)
    table = members.reshape(top, rows).T
    table = table[jax.random.permutation(jax.random.fold_in(own, 1), rows)]
    rotation = jax.random.randint(jax.random.fold_in(own, 2), (rows, 1), 0, top)
    return jnp.take_along_axis(table, (jnp.arange(top)[None, :] + rotation) % top, axis=1)


def portions_of(amount, total, reach, slope, full):
    portions = [(1 << 20) // math.isqrt(standing ** slope) + 1 for standing in range(1, amount + 1)]
    largest = reach if full else min(reach, max(-(-total // amount), total * portions[0] // sum(portions)))
    least = 1 if total - largest >= amount - 1 else 0
    holding, spare = [largest] + [least] * (amount - 1), total - largest - least * (amount - 1)
    while spare > 0:
        free = [i for i in range(1, amount) if holding[i] < largest] or [i for i in range(1, amount) if holding[i] < reach]
        pool, budget = sum([portions[i] for i in free]), spare
        for i in free:
            addition = min(reach - holding[i], max(1, budget * portions[i] // pool), spare)
            holding[i] = holding[i] + addition
            spare = spare - addition
    return np.array(holding)


def centred(key, shape, width, most, shards=(), kind=jnp.bfloat16):
    entries = width * jax.random.normal(key, shape, jnp.float32)
    if shards:
        entries = entries * steps_of(key, shape, shards, -0.22, 0.18)
    return jnp.clip(entries, -most, most).astype(kind)


def setup_inputs(seed: int = 0) -> dict:
    arg_keys = jax.random.split(jax.random.key(seed), 7)
    spectra = centred(arg_keys[0], (STATIONS, 2 * F), 1.0, 6.0, ((0, 512),))
    gap_counts = place_ends(jax.random.randint(arg_keys[1], (STATIONS,), 0, 54000), jax.random.fold_in(arg_keys[1], 1), 0, 53999).astype(jnp.int32)
    band_weight = jnp.clip(jnp.exp(jax.random.uniform(arg_keys[2], (F,), jnp.float32, math.log(0.1), math.log(1.0))), 0.1, 1.0)
    pair_list = draw_pair_list(jax.random.fold_in(arg_keys[6], 71), 0)
    stack_owner_keys = jax.random.split(jax.random.fold_in(arg_keys[4], 1), PAIRS // PAIRS_DEV)
    stack_owner_turns = jax.random.permutation(jax.random.fold_in(arg_keys[4], 3), PAIRS // PAIRS_DEV)
    stack_owner = jax.vmap(lambda own, number: deal_out(jax.random.fold_in(arg_keys[4], 2), own, number, PAIRS_DEV, N_SEG, 1, CAP, 2))(stack_owner_keys, stack_owner_turns).reshape((PAIRS, 1))
    stack_slot = place_ends(jax.random.randint(arg_keys[5], (PAIRS,), 0, SLOTS_DEV), jax.random.fold_in(arg_keys[5], 1), 0, SLOTS_DEV - 1).astype(jnp.int32)
    return dict(spectra=spectra, gap_counts=gap_counts, band_weight=band_weight, pair_list=pair_list, stack_owner=stack_owner, stack_slot=stack_slot)


def whiten(spectra, gap_counts):
    values = spectra.astype(jnp.float32)
    power = lax.optimization_barrier(jnp.mean(values * values, axis=1))
    factor = jnp.sqrt(SAMPLES / (SAMPLES - gap_counts.astype(jnp.float32))) / jnp.sqrt(power + 1e-06)
    return (values * factor[:, None]).astype(jnp.bfloat16)

def make_kernel(band_weight):
    freqs = jnp.arange(F, dtype=jnp.int32)
    shifts = jnp.arange(LAGS, dtype=jnp.int32) - LAGS // 2
    phase_index = freqs[:, None] * shifts[None, :] % (2 * F)
    angles = phase_index.astype(jnp.float32) * (math.pi / F)
    weights = band_weight * (0.25 / math.sqrt(F))
    upper = weights[:, None] * jnp.cos(angles)
    lower = -weights[:, None] * jnp.sin(angles)
    return jnp.concatenate([upper, lower], axis=0).astype(jnp.bfloat16)

def correlate(rows_first, rows_second, kernel):
    half = rows_first.shape[1] // 2
    real_first = rows_first[:, :half].astype(jnp.float32)
    imag_first = rows_first[:, half:].astype(jnp.float32)
    real_second = rows_second[:, :half].astype(jnp.float32)
    imag_second = rows_second[:, half:].astype(jnp.float32)
    cross = jnp.concatenate([real_first * real_second + imag_first * imag_second, imag_first * real_second - real_first * imag_second], axis=1).astype(jnp.bfloat16)
    return jnp.dot(cross, kernel, preferred_element_type=jnp.float32)

def reference(spectra, gap_counts, band_weight, pair_list, stack_owner, stack_slot):
    white = whiten(spectra, gap_counts)
    kernel = make_kernel(band_weight)
    total = pair_list.shape[0]
    block_index = jnp.arange(total, dtype=jnp.int32) // PAIRS_DEV
    seg_index = block_index % N_SEG
    grp_index = block_index // N_SEG

    def globalize(local):
        return (local // S_DEV * N_SEG + seg_index) * S_DEV + local % S_DEV
    first = globalize(pair_list[:, 0]).astype(jnp.int32)
    second = globalize(pair_list[:, 1]).astype(jnp.int32)
    targets = ((grp_index * N_SEG + stack_owner[:, 0]) * SLOTS_DEV + stack_slot).astype(jnp.int32)
    rows = min(4096, total)
    count = total // rows
    bins_all = N_GRP * N_SEG * SLOTS_DEV

    def step(accum, packed):
        left, right, where = packed
        corr = correlate(white[left], white[right], kernel)
        return (accum + jax.ops.segment_sum(corr, where, bins_all), None)
    start = jnp.zeros((bins_all, LAGS), jnp.float32)
    stacked, _ = lax.scan(step, start, (first.reshape(count, rows), second.reshape(count, rows), targets.reshape(count, rows)))
    return stacked
```

```python
import math

import jax
import jax.numpy as jnp
import numpy as np
from jax import lax
from jax.experimental import pallas as pl
from jax.experimental.pallas import tpu as pltpu
from jax.sharding import PartitionSpec as P

F = 2048
LAGS = 256
SAMPLES = 72000
SLOTS_DEV = 32
LIFT = 256.0
CHUNK = 512
ROWS = 256
VMEM = 56 * 1024 * 1024


def tables():
    freqs = np.arange(F, dtype=np.int64)
    shifts = np.arange(LAGS, dtype=np.int64) - LAGS // 2
    angles = ((shifts[:, None] * freqs[None, :]) % (2 * F)).astype(np.float64) * (math.pi / F)
    return np.cos(angles).astype(np.float32), (-np.sin(angles)).astype(np.float32)


def whiten_kernel(spectra_ref, gap_ref, out_ref):
    values = spectra_ref[...].astype(jnp.float32)
    power = jnp.mean(values * values, axis=1, keepdims=True)
    kept = SAMPLES - gap_ref[...].astype(jnp.float32)
    factor = jnp.sqrt(SAMPLES / kept) / jnp.sqrt(power + 1e-06)
    out_ref[...] = (values * factor).astype(jnp.bfloat16) * LIFT


def pick_bins(owner_ref, slot_ref, parity):
    owner = owner_ref[...]
    local = (owner >> 1) * SLOTS_DEV + slot_ref[...]
    return jnp.where((owner & 1) == parity, local, -1)


def into_bins(bins, corr_ref, out_ref):
    pairs = corr_ref.shape[0]
    count = out_ref.shape[0]
    for start in range(0, count, ROWS):
        ids = lax.broadcasted_iota(jnp.int32, (ROWS, pairs), 0) + start
        place = (ids == bins).astype(jnp.bfloat16)
        out_ref[start : start + ROWS, :] = jnp.dot(
            place, corr_ref[...], preferred_element_type=jnp.float32
        ).astype(out_ref.dtype)


def correlate_kernel(
    pairs_ref, owner_ref, slot_ref, real_ref, imag_ref, weight_ref, cos_ref, sin_ref,
    corr_ref, away_ref, first_ref, second_ref, total_ref,
):
    step = pl.program_id(0)
    group = real_ref.shape[0]
    pairs = total_ref.shape[0]

    @pl.when(step == 0)
    def _():
        ids = lax.broadcasted_iota(jnp.int32, (group, pairs), 0)
        first_ref[...] = (ids == pairs_ref[0:1, :]).astype(jnp.float32).T.astype(jnp.bfloat16)
        second_ref[...] = (ids == pairs_ref[1:2, :]).astype(jnp.float32).T.astype(jnp.bfloat16)
        total_ref[...] = jnp.zeros_like(total_ref)

    weight = weight_ref[...] * (0.25 / math.sqrt(F) / (LIFT * LIFT))
    upper = (weight * cos_ref[...]).astype(jnp.bfloat16)
    lower = (weight * sin_ref[...]).astype(jnp.bfloat16)
    real = real_ref[...]
    imag = imag_ref[...]

    def pick(one_hot, rows):
        return jnp.dot(one_hot, rows, preferred_element_type=jnp.float32)

    def lags(cross, table):
        return lax.dot_general(
            cross.astype(jnp.bfloat16), table, (((1,), (1,)), ((), ())),
            preferred_element_type=jnp.float32,
        )

    for start in range(0, pairs, ROWS):
        rows = slice(start, start + ROWS)
        one, two = first_ref[rows, :], second_ref[rows, :]
        real_one, imag_one = pick(one, real), pick(one, imag)
        real_two, imag_two = pick(two, real), pick(two, imag)
        total_ref[rows, :] += lags(real_one * real_two + imag_one * imag_two, upper) + lags(
            imag_one * real_two - real_one * imag_two, lower
        )

    @pl.when(step == pl.num_programs(0) - 1)
    def _():
        corr_ref[...] = total_ref[...].astype(jnp.bfloat16)
        core = lax.axis_index("seg") & 1
        into_bins(pick_bins(owner_ref, slot_ref, 1 - core), corr_ref, away_ref)


def own_kernel(owner_ref, slot_ref, corr_ref, out_ref):
    core = lax.axis_index("seg") & 1
    into_bins(pick_bins(owner_ref, slot_ref, core), corr_ref, out_ref)


def on_device(spectra, gap_counts, band_weight, pair_list, stack_owner, stack_slot):
    stations = spectra.shape[0]
    pairs = pair_list.shape[0]
    seg = lax.axis_size("seg")
    group = stations * lax.axis_size("grp")
    bins = seg // 2 * SLOTS_DEV
    steps = F // CHUNK
    params = pltpu.CompilerParams(vmem_limit_bytes=VMEM)
    white = pl.pallas_call(
        whiten_kernel, out_shape=jax.ShapeDtypeStruct(spectra.shape, jnp.bfloat16), compiler_params=params
    )(spectra, gap_counts.reshape(stations, 1))
    group_rows = lax.all_gather(white.astype(jnp.float16), "grp", axis=0, tiled=True).astype(jnp.bfloat16)

    owner = stack_owner.reshape(1, pairs)
    slot = stack_slot.reshape(1, pairs)
    cos_table, sin_table = tables()
    whole = lambda rows, columns: pl.BlockSpec((rows, columns), lambda i: (0, 0))
    corr, away = pl.pallas_call(
        correlate_kernel,
        grid=(steps,),
        in_specs=[
            whole(2, pairs),
            whole(1, pairs),
            whole(1, pairs),
            pl.BlockSpec((group, CHUNK), lambda i: (0, i)),
            pl.BlockSpec((group, CHUNK), lambda i: (0, i + steps)),
            pl.BlockSpec((1, CHUNK), lambda i: (0, i)),
            pl.BlockSpec((LAGS, CHUNK), lambda i: (0, i)),
            pl.BlockSpec((LAGS, CHUNK), lambda i: (0, i)),
        ],
        out_specs=[whole(pairs, LAGS), whole(bins, LAGS)],
        out_shape=[
            jax.ShapeDtypeStruct((pairs, LAGS), jnp.bfloat16),
            jax.ShapeDtypeStruct((bins, LAGS), jnp.bfloat16),
        ],
        scratch_shapes=[
            pltpu.VMEM((pairs, group), jnp.bfloat16),
            pltpu.VMEM((pairs, group), jnp.bfloat16),
            pltpu.VMEM((pairs, LAGS), jnp.float32),
        ],
        compiler_params=params,
    )(
        pair_list.T, owner, slot, group_rows, group_rows, band_weight.reshape(1, F), cos_table, sin_table
    )
    arrived = lax.ppermute(away, "seg", [(i, i ^ 1) for i in range(seg)])
    kept = pl.pallas_call(
        own_kernel,
        out_shape=jax.ShapeDtypeStruct((bins, LAGS), jnp.float32),
        compiler_params=params,
        cost_estimate=pl.CostEstimate(flops=2 * bins * pairs * LAGS, bytes_accessed=2 << 20, transcendentals=0),
    )(owner, slot, corr)
    chip = (kept + arrived.astype(jnp.float32)).astype(jnp.bfloat16).reshape(seg // 2, SLOTS_DEV, LAGS)
    got = lax.all_to_all(
        chip, "seg", split_axis=0, concat_axis=0, tiled=True,
        axis_index_groups=[list(range(core, seg, 2)) for core in range(2)],
    )
    return jnp.sum(got.astype(jnp.float32), axis=0)


def solution(mesh):
    placed = (
        P(("grp", "seg"), None),
        P(("grp", "seg")),
        P(),
        P(("grp", "seg"), None),
        P(("grp", "seg"), None),
        P(("grp", "seg")),
    )
    return jax.shard_map(
        on_device, mesh=mesh, in_specs=placed, out_specs=P(("grp", "seg"), None), check_vma=False
    )
```

```python
import math

import jax
import jax.numpy as jnp
import numpy as np
from jax import lax
from jax.experimental import pallas as pl
from jax.experimental.pallas import tpu as pltpu
from jax.sharding import PartitionSpec as P

F = 2048
LAGS = 256
SAMPLES = 72000
SLOTS_DEV = 32
LIFT = 256.0
COLUMNS = 256
ROWS = 512
BIN_ROWS = 256
MIB = 1024 * 1024


def tables():
    freqs = np.arange(F, dtype=np.int64)
    shifts = np.arange(LAGS, dtype=np.int64) - LAGS // 2
    angles = ((shifts[:, None] * freqs[None, :]) % (2 * F)).astype(np.float64) * (math.pi / F)
    return np.cos(angles).astype(np.float32), (-np.sin(angles)).astype(np.float32)


def whiten_kernel(spectra_ref, gap_ref, out_ref):
    stations = spectra_ref.shape[0]
    values = spectra_ref[...].astype(jnp.float32)
    power = jnp.mean(values * values, axis=1, keepdims=True)
    kept = jnp.broadcast_to(SAMPLES - gap_ref[...].astype(jnp.float32), (stations, stations))
    here = lax.broadcasted_iota(jnp.int32, (stations, stations), 0)
    along = lax.broadcasted_iota(jnp.int32, (stations, stations), 1)
    kept = jnp.sum(jnp.where(here == along, kept, 0.0), axis=1, keepdims=True)
    factor = jnp.sqrt(SAMPLES / kept) / jnp.sqrt(power + 1e-06)
    out_ref[...] = (values * factor).astype(jnp.bfloat16) * LIFT


def pick_bins(owner_ref, slot_ref, parity):
    owner = owner_ref[...]
    local = (owner >> 1) * SLOTS_DEV + slot_ref[...]
    return jnp.where((owner & 1) == parity, local, -1)


def into_bins(bins, corr_ref, out_ref):
    pairs = corr_ref.shape[0]
    count = out_ref.shape[0]
    for start in range(0, count, BIN_ROWS):
        ids = lax.broadcasted_iota(jnp.int32, (BIN_ROWS, pairs), 0) + start
        place = (ids == bins).astype(jnp.bfloat16)
        out_ref[start : start + BIN_ROWS, :] = jnp.dot(
            place, corr_ref[...], preferred_element_type=jnp.float32
        ).astype(out_ref.dtype)


def correlate_kernel(
    pairs_ref, owner_ref, slot_ref, white_ref, weight_ref, cos_ref, sin_ref,
    corr_ref, away_ref, first_ref, second_ref, upper_ref, lower_ref,
):
    group = white_ref.shape[0]
    pairs = corr_ref.shape[0]
    ids = lax.broadcasted_iota(jnp.int32, (group, pairs), 0)
    first_ref[...] = (ids == pairs_ref[0:1, :]).astype(jnp.float32).T.astype(jnp.bfloat16)
    second_ref[...] = (ids == pairs_ref[1:2, :]).astype(jnp.float32).T.astype(jnp.bfloat16)
    weight = weight_ref[...] * (0.25 / math.sqrt(F) / (LIFT * LIFT))
    upper_ref[...] = (weight * cos_ref[...]).astype(jnp.bfloat16)
    lower_ref[...] = (weight * sin_ref[...]).astype(jnp.bfloat16)

    def pick(one_hot, rows):
        return jnp.dot(one_hot, rows, preferred_element_type=jnp.float32)

    def lags(cross, table):
        return lax.dot_general(
            cross.astype(jnp.bfloat16), table, (((1,), (1,)), ((), ())),
            preferred_element_type=jnp.float32,
        )

    for start in range(0, pairs, ROWS):
        rows = slice(start, start + ROWS)
        one, two = first_ref[rows, :], second_ref[rows, :]
        total = jnp.zeros((ROWS, LAGS), jnp.float32)
        for column in range(0, F, COLUMNS):
            here = slice(column, column + COLUMNS)
            real = white_ref[:, here]
            imag = white_ref[:, F + column : F + column + COLUMNS]
            real_one, imag_one = pick(one, real), pick(one, imag)
            real_two, imag_two = pick(two, real), pick(two, imag)
            total += lags(real_one * real_two + imag_one * imag_two, upper_ref[:, here]) + lags(
                imag_one * real_two - real_one * imag_two, lower_ref[:, here]
            )
        corr_ref[rows, :] = total.astype(jnp.bfloat16)
    core = lax.axis_index("seg") & 1
    into_bins(pick_bins(owner_ref, slot_ref, 1 - core), corr_ref, away_ref)


def own_kernel(owner_ref, slot_ref, corr_ref, out_ref):
    core = lax.axis_index("seg") & 1
    into_bins(pick_bins(owner_ref, slot_ref, core), corr_ref, out_ref)


def on_device(spectra, gap_counts, band_weight, pair_list, stack_owner, stack_slot):
    stations = spectra.shape[0]
    pairs = pair_list.shape[0]
    seg = lax.axis_size("seg")
    group = stations * lax.axis_size("grp")
    bins = seg // 2 * SLOTS_DEV
    white = pl.pallas_call(
        whiten_kernel,
        out_shape=jax.ShapeDtypeStruct(spectra.shape, jnp.bfloat16),
        compiler_params=pltpu.CompilerParams(vmem_limit_bytes=8 * MIB),
    )(spectra, gap_counts.reshape(1, stations))
    group_rows = lax.all_gather(white.astype(jnp.float16), "grp", axis=0, tiled=True).astype(jnp.bfloat16)

    owner = stack_owner.reshape(1, pairs)
    slot = stack_slot.reshape(1, pairs)
    cos_table, sin_table = tables()
    corr, away = pl.pallas_call(
        correlate_kernel,
        out_shape=[
            jax.ShapeDtypeStruct((pairs, LAGS), jnp.bfloat16),
            jax.ShapeDtypeStruct((bins, LAGS), jnp.bfloat16),
        ],
        scratch_shapes=[
            pltpu.VMEM((pairs, group), jnp.bfloat16),
            pltpu.VMEM((pairs, group), jnp.bfloat16),
            pltpu.VMEM((LAGS, F), jnp.bfloat16),
            pltpu.VMEM((LAGS, F), jnp.bfloat16),
        ],
        compiler_params=pltpu.CompilerParams(vmem_limit_bytes=24 * MIB),
    )(
        pair_list.T, owner, slot, group_rows, band_weight.reshape(1, F), cos_table, sin_table
    )
    arrived = lax.ppermute(away, "seg", [(i, i ^ 1) for i in range(seg)])
    kept = pl.pallas_call(
        own_kernel,
        out_shape=jax.ShapeDtypeStruct((bins, LAGS), jnp.float32),
        compiler_params=pltpu.CompilerParams(vmem_limit_bytes=8 * MIB),
        cost_estimate=pl.CostEstimate(flops=2 * bins * pairs * LAGS, bytes_accessed=2 << 20, transcendentals=0),
    )(owner, slot, corr)
    chip = (kept + arrived.astype(jnp.float32)).astype(jnp.bfloat16).reshape(seg // 2, SLOTS_DEV, LAGS)
    got = lax.all_to_all(
        chip, "seg", split_axis=0, concat_axis=0, tiled=True,
        axis_index_groups=[list(range(core, seg, 2)) for core in range(2)],
    )
    return jnp.sum(got.astype(jnp.float32), axis=0)


def solution(mesh):
    placed = (
        P(("grp", "seg"), None),
        P(("grp", "seg")),
        P(),
        P(("grp", "seg"), None),
        P(("grp", "seg"), None),
        P(("grp", "seg")),
    )
    return jax.shard_map(
        on_device, mesh=mesh, in_specs=placed, out_specs=P(("grp", "seg"), None), check_vma=False
    )
```

```python
import math

import jax
import jax.numpy as jnp
import numpy as np
from jax import lax
from jax.experimental import pallas as pl
from jax.experimental.pallas import tpu as pltpu
from jax.sharding import PartitionSpec as P

F = 2048
LAGS = 256
SAMPLES = 72000
SLOTS_DEV = 32
LIFT = 256.0
FINE = 16
COLUMNS = 256
ROWS = 512
BIN_ROWS = 256
MIB = 1024 * 1024


def tables():
    freqs = np.arange(F, dtype=np.int64)
    coarse = np.arange(0, LAGS, FINE, dtype=np.int64) - LAGS // 2
    fine = np.arange(FINE, dtype=np.int64)
    angles = [(k[:, None] * freqs[None, :]) % (2 * F) * (math.pi / F) for k in (coarse, fine)]
    return [f(angle).astype(np.float32) for angle in angles for f in (np.cos, np.sin)]


def whiten_kernel(spectra_ref, gap_ref, out_ref):
    stations = spectra_ref.shape[0]
    values = spectra_ref[...].astype(jnp.float32)
    power = jnp.mean(values * values, axis=1, keepdims=True)
    kept = jnp.broadcast_to(SAMPLES - gap_ref[...].astype(jnp.float32), (stations, stations))
    here = lax.broadcasted_iota(jnp.int32, (stations, stations), 0)
    along = lax.broadcasted_iota(jnp.int32, (stations, stations), 1)
    kept = jnp.sum(jnp.where(here == along, kept, 0.0), axis=1, keepdims=True)
    factor = jnp.sqrt(SAMPLES / kept) / jnp.sqrt(power + 1e-06)
    out_ref[...] = (values * factor).astype(jnp.bfloat16) * LIFT


def pick_bins(owner_ref, slot_ref, parity):
    owner = owner_ref[...]
    local = (owner >> 1) * SLOTS_DEV + slot_ref[...]
    return jnp.where((owner & 1) == parity, local, -1)


def into_bins(bins, corr_ref, out_ref):
    pairs = corr_ref.shape[0]
    count = out_ref.shape[0]
    for start in range(0, count, BIN_ROWS):
        ids = lax.broadcasted_iota(jnp.int32, (BIN_ROWS, pairs), 0) + start
        place = (ids == bins).astype(jnp.bfloat16)
        out_ref[start : start + BIN_ROWS, :] = jnp.dot(
            place, corr_ref[...], preferred_element_type=jnp.float32
        ).astype(out_ref.dtype)


def correlate_kernel(
    pairs_ref, owner_ref, slot_ref, white_ref, weight_ref, cos_ref, sin_ref, cos_fine_ref, sin_fine_ref,
    corr_ref, away_ref, first_ref, second_ref, table_ref,
):
    group = white_ref.shape[0]
    pairs = corr_ref.shape[0]
    ids = lax.broadcasted_iota(jnp.int32, (group, pairs), 0)
    first_ref[...] = (ids == pairs_ref[0:1, :]).astype(jnp.float32).T.astype(jnp.bfloat16)
    second_ref[...] = (ids == pairs_ref[1:2, :]).astype(jnp.float32).T.astype(jnp.bfloat16)
    weight = weight_ref[...] * (0.25 / math.sqrt(F) / (LIFT * LIFT))
    for lag in range(0, LAGS, FINE):
        cos = weight * cos_ref[lag // FINE : lag // FINE + 1, :]
        sin = weight * sin_ref[lag // FINE : lag // FINE + 1, :]
        upper = (cos * cos_fine_ref[...] - sin * sin_fine_ref[...]).astype(jnp.bfloat16)
        lower = (-(sin * cos_fine_ref[...] + cos * sin_fine_ref[...])).astype(jnp.bfloat16)
        for column in range(0, F, COLUMNS):
            here = slice(column, column + COLUMNS)
            table_ref[lag : lag + FINE, 2 * column : 2 * column + COLUMNS] = upper[:, here]
            table_ref[lag : lag + FINE, 2 * column + COLUMNS : 2 * column + 2 * COLUMNS] = lower[:, here]

    def pick(one_hot, rows):
        return jnp.dot(one_hot, rows, preferred_element_type=jnp.float32)

    def lags(cross, table):
        return lax.dot_general(
            cross, table, (((1,), (1,)), ((), ())), preferred_element_type=jnp.float32
        )

    for start in range(0, pairs, ROWS):
        rows = slice(start, start + ROWS)
        one, two = first_ref[rows, :], second_ref[rows, :]
        total = jnp.zeros((ROWS, LAGS), jnp.float32)
        for column in range(0, F, COLUMNS):
            here = slice(column, column + COLUMNS)
            real = white_ref[:, here]
            imag = white_ref[:, F + column : F + column + COLUMNS]
            real_one, imag_one = pick(one, real), pick(one, imag)
            real_two, imag_two = pick(two, real), pick(two, imag)
            cross = jnp.concatenate(
                [
                    (real_one * real_two + imag_one * imag_two).astype(jnp.bfloat16),
                    (imag_one * real_two - real_one * imag_two).astype(jnp.bfloat16),
                ],
                axis=1,
            )
            total += lags(cross, table_ref[:, 2 * column : 2 * column + 2 * COLUMNS])
        corr_ref[rows, :] = total.astype(jnp.bfloat16)
    core = lax.axis_index("seg") & 1
    into_bins(pick_bins(owner_ref, slot_ref, 1 - core), corr_ref, away_ref)


def own_kernel(owner_ref, slot_ref, corr_ref, out_ref):
    core = lax.axis_index("seg") & 1
    into_bins(pick_bins(owner_ref, slot_ref, core), corr_ref, out_ref)


def on_device(spectra, gap_counts, band_weight, pair_list, stack_owner, stack_slot):
    stations = spectra.shape[0]
    pairs = pair_list.shape[0]
    seg = lax.axis_size("seg")
    group = stations * lax.axis_size("grp")
    bins = seg // 2 * SLOTS_DEV
    white = pl.pallas_call(
        whiten_kernel,
        out_shape=jax.ShapeDtypeStruct(spectra.shape, jnp.bfloat16),
        compiler_params=pltpu.CompilerParams(vmem_limit_bytes=8 * MIB),
    )(spectra, gap_counts.reshape(1, stations))
    group_rows = lax.all_gather(white.astype(jnp.float16), "grp", axis=0, tiled=True).astype(jnp.bfloat16)

    owner = stack_owner.reshape(1, pairs)
    slot = stack_slot.reshape(1, pairs)
    corr, away = pl.pallas_call(
        correlate_kernel,
        out_shape=[
            jax.ShapeDtypeStruct((pairs, LAGS), jnp.bfloat16),
            jax.ShapeDtypeStruct((bins, LAGS), jnp.bfloat16),
        ],
        scratch_shapes=[
            pltpu.VMEM((pairs, group), jnp.bfloat16),
            pltpu.VMEM((pairs, group), jnp.bfloat16),
            pltpu.VMEM((LAGS, 2 * F), jnp.bfloat16),
        ],
        compiler_params=pltpu.CompilerParams(vmem_limit_bytes=24 * MIB),
    )(
        pair_list.T, owner, slot, group_rows, band_weight.reshape(1, F), *tables()
    )
    arrived = lax.ppermute(away, "seg", [(i, i ^ 1) for i in range(seg)])
    kept = pl.pallas_call(
        own_kernel,
        out_shape=jax.ShapeDtypeStruct((bins, LAGS), jnp.float32),
        compiler_params=pltpu.CompilerParams(vmem_limit_bytes=8 * MIB),
        cost_estimate=pl.CostEstimate(flops=2 * bins * pairs * LAGS, bytes_accessed=2 << 20, transcendentals=0),
    )(owner, slot, corr)
    chip = (kept + arrived.astype(jnp.float32)).astype(jnp.bfloat16).reshape(seg // 2, SLOTS_DEV, LAGS)
    got = lax.all_to_all(
        chip, "seg", split_axis=0, concat_axis=0, tiled=True,
        axis_index_groups=[list(range(core, seg, 2)) for core in range(2)],
    )
    return jnp.sum(got.astype(jnp.float32), axis=0)


def solution(mesh):
    placed = (
        P(("grp", "seg"), None),
        P(("grp", "seg")),
        P(),
        P(("grp", "seg"), None),
        P(("grp", "seg"), None),
        P(("grp", "seg")),
    )
    return jax.shard_map(
        on_device, mesh=mesh, in_specs=placed, out_specs=P(("grp", "seg"), None), check_vma=False
    )
```

```python
import math

import jax
import jax.numpy as jnp
import numpy as np
from jax import lax
from jax.experimental import pallas as pl
from jax.experimental.pallas import tpu as pltpu
from jax.sharding import PartitionSpec as P

F = 2048
LAGS = 256
SAMPLES = 72000
SLOTS_DEV = 32
LIFT = 256.0
FINE = 16
COLUMNS = 256
ROWS = 512
BIN_ROWS = 256
MIB = 1024 * 1024


def tables():
    freqs = np.arange(F, dtype=np.int64)
    coarse = np.arange(0, LAGS, FINE, dtype=np.int64) - LAGS // 2
    fine = np.arange(FINE, dtype=np.int64)
    angles = [(k[:, None] * freqs[None, :]) % (2 * F) * (math.pi / F) for k in (coarse, fine)]
    return [f(angle).astype(np.float32) for angle in angles for f in (np.cos, np.sin)]


def whiten(spectra, gap_counts):
    values = spectra.astype(jnp.float32)
    power = jnp.mean(values * values, axis=1)
    factor = jnp.sqrt(SAMPLES / (SAMPLES - gap_counts.astype(jnp.float32))) / jnp.sqrt(power + 1e-06)
    return (values * factor[:, None]).astype(jnp.bfloat16)


def pick_bins(owner_ref, slot_ref, parity):
    owner = owner_ref[...]
    local = (owner >> 1) * SLOTS_DEV + slot_ref[...]
    return jnp.where((owner & 1) == parity, local, -1)


def into_bins(bins, corr_ref, out_ref):
    pairs = corr_ref.shape[0]
    count = out_ref.shape[0]
    for start in range(0, count, BIN_ROWS):
        ids = lax.broadcasted_iota(jnp.int32, (BIN_ROWS, pairs), 0) + start
        place = (ids == bins).astype(jnp.bfloat16)
        out_ref[start : start + BIN_ROWS, :] = jnp.dot(
            place, corr_ref[...], preferred_element_type=jnp.float32
        ).astype(out_ref.dtype)


def correlate_kernel(
    pairs_ref, owner_ref, slot_ref, white_ref, weight_ref, cos_ref, sin_ref, cos_fine_ref, sin_fine_ref,
    corr_ref, away_ref, first_ref, second_ref, table_ref,
):
    group = white_ref.shape[0]
    pairs = corr_ref.shape[0]
    ids = lax.broadcasted_iota(jnp.int32, (group, pairs), 0)
    first_ref[...] = (ids == pairs_ref[0:1, :]).astype(jnp.float32).T.astype(jnp.bfloat16)
    second_ref[...] = (ids == pairs_ref[1:2, :]).astype(jnp.float32).T.astype(jnp.bfloat16)
    weight = weight_ref[...] * (0.25 / math.sqrt(F) / (LIFT * LIFT))
    for lag in range(0, LAGS, FINE):
        cos = weight * cos_ref[lag // FINE : lag // FINE + 1, :]
        sin = weight * sin_ref[lag // FINE : lag // FINE + 1, :]
        upper = (cos * cos_fine_ref[...] - sin * sin_fine_ref[...]).astype(jnp.bfloat16)
        lower = (-(sin * cos_fine_ref[...] + cos * sin_fine_ref[...])).astype(jnp.bfloat16)
        for column in range(0, F, COLUMNS):
            here = slice(column, column + COLUMNS)
            table_ref[lag : lag + FINE, 2 * column : 2 * column + COLUMNS] = upper[:, here]
            table_ref[lag : lag + FINE, 2 * column + COLUMNS : 2 * column + 2 * COLUMNS] = lower[:, here]

    def pick(one_hot, rows):
        return jnp.dot(one_hot, rows, preferred_element_type=jnp.float32)

    def lags(cross, table):
        return lax.dot_general(
            cross, table, (((1,), (1,)), ((), ())), preferred_element_type=jnp.float32
        )

    for start in range(0, pairs, ROWS):
        rows = slice(start, start + ROWS)
        one, two = first_ref[rows, :], second_ref[rows, :]
        total = jnp.zeros((ROWS, LAGS), jnp.float32)
        for column in range(0, F, COLUMNS):
            here = slice(column, column + COLUMNS)
            real = white_ref[:, here]
            imag = white_ref[:, F + column : F + column + COLUMNS]
            real_one, imag_one = pick(one, real), pick(one, imag)
            real_two, imag_two = pick(two, real), pick(two, imag)
            cross = jnp.concatenate(
                [
                    (real_one * real_two + imag_one * imag_two).astype(jnp.bfloat16),
                    (imag_one * real_two - real_one * imag_two).astype(jnp.bfloat16),
                ],
                axis=1,
            )
            total += lags(cross, table_ref[:, 2 * column : 2 * column + 2 * COLUMNS])
        corr_ref[rows, :] = total.astype(jnp.bfloat16)
    core = lax.axis_index("seg") & 1
    into_bins(pick_bins(owner_ref, slot_ref, 1 - core), corr_ref, away_ref)


def own_kernel(owner_ref, slot_ref, corr_ref, out_ref):
    core = lax.axis_index("seg") & 1
    into_bins(pick_bins(owner_ref, slot_ref, core), corr_ref, out_ref)


def on_device(spectra, gap_counts, band_weight, pair_list, stack_owner, stack_slot):
    stations = spectra.shape[0]
    pairs = pair_list.shape[0]
    seg = lax.axis_size("seg")
    group = stations * lax.axis_size("grp")
    bins = seg // 2 * SLOTS_DEV
    lifted = (whiten(spectra, gap_counts) * LIFT).astype(jnp.float16)
    group_rows = lax.all_gather(lifted, "grp", axis=0, tiled=True).astype(jnp.bfloat16)

    owner = stack_owner.reshape(1, pairs)
    slot = stack_slot.reshape(1, pairs)
    corr, away = pl.pallas_call(
        correlate_kernel,
        out_shape=[
            jax.ShapeDtypeStruct((pairs, LAGS), jnp.bfloat16),
            jax.ShapeDtypeStruct((bins, LAGS), jnp.bfloat16),
        ],
        scratch_shapes=[
            pltpu.VMEM((pairs, group), jnp.bfloat16),
            pltpu.VMEM((pairs, group), jnp.bfloat16),
            pltpu.VMEM((LAGS, 2 * F), jnp.bfloat16),
        ],
        compiler_params=pltpu.CompilerParams(vmem_limit_bytes=24 * MIB),
    )(
        pair_list.T, owner, slot, group_rows, band_weight.reshape(1, F), *tables()
    )
    arrived = lax.ppermute(away, "seg", [(i, i ^ 1) for i in range(seg)])
    kept = pl.pallas_call(
        own_kernel,
        out_shape=jax.ShapeDtypeStruct((bins, LAGS), jnp.float32),
        compiler_params=pltpu.CompilerParams(vmem_limit_bytes=8 * MIB),
        cost_estimate=pl.CostEstimate(flops=2 * bins * pairs * LAGS, bytes_accessed=2 << 20, transcendentals=0),
    )(owner, slot, corr)
    chip = (kept + arrived.astype(jnp.float32)).astype(jnp.bfloat16).reshape(seg // 2, SLOTS_DEV, LAGS)
    got = lax.all_to_all(
        chip, "seg", split_axis=0, concat_axis=0, tiled=True,
        axis_index_groups=[list(range(core, seg, 2)) for core in range(2)],
    )
    return jnp.sum(got.astype(jnp.float32), axis=0)


def solution(mesh):
    placed = (
        P(("grp", "seg"), None),
        P(("grp", "seg")),
        P(),
        P(("grp", "seg"), None),
        P(("grp", "seg"), None),
        P(("grp", "seg")),
    )
    return jax.shard_map(
        on_device, mesh=mesh, in_specs=placed, out_specs=P(("grp", "seg"), None), check_vma=False
    )
```

```python
import math

import jax
import jax.numpy as jnp
import numpy as np
from jax import lax
from jax.experimental import pallas as pl
from jax.experimental.pallas import tpu as pltpu
from jax.sharding import PartitionSpec as P

F = 2048
LAGS = 256
SAMPLES = 72000
SLOTS_DEV = 32
CHIPS_Y, CHIPS_X = 8, 4
LIFT = 256.0
FINE = 16
COLUMNS = 256
ROWS = 512
BIN_ROWS = 256
MIB = 1024 * 1024


def tables():
    freqs = np.arange(F, dtype=np.int64)
    coarse = np.arange(0, LAGS, FINE, dtype=np.int64) - LAGS // 2
    fine = np.arange(FINE, dtype=np.int64)
    angles = [(k[:, None] * freqs[None, :]) % (2 * F) * (math.pi / F) for k in (coarse, fine)]
    return [f(angle).astype(np.float32) for angle in angles for f in (np.cos, np.sin)]


def whiten_kernel(spectra_ref, gap_ref, out_ref):
    stations = spectra_ref.shape[0]
    values = spectra_ref[...].astype(jnp.float32)
    power = jnp.mean(values * values, axis=1, keepdims=True)
    kept = jnp.broadcast_to(SAMPLES - gap_ref[...].astype(jnp.float32), (stations, stations))
    here = lax.broadcasted_iota(jnp.int32, (stations, stations), 0)
    along = lax.broadcasted_iota(jnp.int32, (stations, stations), 1)
    kept = jnp.sum(jnp.where(here == along, kept, 0.0), axis=1, keepdims=True)
    factor = jnp.sqrt(SAMPLES / kept) / jnp.sqrt(power + 1e-06)
    out_ref[...] = (values * factor).astype(jnp.bfloat16) * LIFT


def pick_bins(owner_ref, slot_ref, parity):
    owner = owner_ref[...]
    chip = owner >> 1
    local = ((chip % CHIPS_X) * CHIPS_Y + chip // CHIPS_X) * SLOTS_DEV + slot_ref[...]
    return jnp.where((owner & 1) == parity, local, -1)


def into_bins(bins, corr_ref, out_ref):
    pairs = corr_ref.shape[0]
    count = out_ref.shape[0]
    for start in range(0, count, BIN_ROWS):
        ids = lax.broadcasted_iota(jnp.int32, (BIN_ROWS, pairs), 0) + start
        place = (ids == bins).astype(jnp.bfloat16)
        out_ref[start : start + BIN_ROWS, :] = jnp.dot(
            place, corr_ref[...], preferred_element_type=jnp.float32
        ).astype(out_ref.dtype)


def correlate_kernel(
    pairs_ref, owner_ref, slot_ref, white_ref, weight_ref, cos_ref, sin_ref, cos_fine_ref, sin_fine_ref,
    corr_ref, away_ref, first_ref, second_ref, table_ref,
):
    group = white_ref.shape[0]
    pairs = corr_ref.shape[0]
    ids = lax.broadcasted_iota(jnp.int32, (group, pairs), 0)
    first_ref[...] = (ids == pairs_ref[0:1, :]).astype(jnp.float32).T.astype(jnp.bfloat16)
    second_ref[...] = (ids == pairs_ref[1:2, :]).astype(jnp.float32).T.astype(jnp.bfloat16)
    weight = weight_ref[...] * (0.25 / math.sqrt(F) / (LIFT * LIFT))
    for lag in range(0, LAGS, FINE):
        cos = weight * cos_ref[lag // FINE : lag // FINE + 1, :]
        sin = weight * sin_ref[lag // FINE : lag // FINE + 1, :]
        upper = (cos * cos_fine_ref[...] - sin * sin_fine_ref[...]).astype(jnp.bfloat16)
        lower = (-(sin * cos_fine_ref[...] + cos * sin_fine_ref[...])).astype(jnp.bfloat16)
        for column in range(0, F, COLUMNS):
            here = slice(column, column + COLUMNS)
            table_ref[lag : lag + FINE, 2 * column : 2 * column + COLUMNS] = upper[:, here]
            table_ref[lag : lag + FINE, 2 * column + COLUMNS : 2 * column + 2 * COLUMNS] = lower[:, here]

    def pick(one_hot, rows):
        return jnp.dot(one_hot, rows, preferred_element_type=jnp.float32)

    def lags(cross, table):
        return lax.dot_general(
            cross, table, (((1,), (1,)), ((), ())), preferred_element_type=jnp.float32
        )

    for start in range(0, pairs, ROWS):
        rows = slice(start, start + ROWS)
        one, two = first_ref[rows, :], second_ref[rows, :]
        total = jnp.zeros((ROWS, LAGS), jnp.float32)
        for column in range(0, F, COLUMNS):
            here = slice(column, column + COLUMNS)
            real = white_ref[:, here]
            imag = white_ref[:, F + column : F + column + COLUMNS]
            real_one, imag_one = pick(one, real), pick(one, imag)
            real_two, imag_two = pick(two, real), pick(two, imag)
            cross = jnp.concatenate(
                [
                    (real_one * real_two + imag_one * imag_two).astype(jnp.bfloat16),
                    (imag_one * real_two - real_one * imag_two).astype(jnp.bfloat16),
                ],
                axis=1,
            )
            total += lags(cross, table_ref[:, 2 * column : 2 * column + 2 * COLUMNS])
        corr_ref[rows, :] = total.astype(jnp.bfloat16)
    core = lax.axis_index("seg") & 1
    into_bins(pick_bins(owner_ref, slot_ref, 1 - core), corr_ref, away_ref)


def own_kernel(owner_ref, slot_ref, corr_ref, out_ref):
    core = lax.axis_index("seg") & 1
    into_bins(pick_bins(owner_ref, slot_ref, core), corr_ref, out_ref)


def on_device(spectra, gap_counts, band_weight, pair_list, stack_owner, stack_slot):
    stations = spectra.shape[0]
    pairs = pair_list.shape[0]
    seg = lax.axis_size("seg")
    group = stations * lax.axis_size("grp")
    bins = seg // 2 * SLOTS_DEV
    white = pl.pallas_call(
        whiten_kernel,
        out_shape=jax.ShapeDtypeStruct(spectra.shape, jnp.bfloat16),
        compiler_params=pltpu.CompilerParams(vmem_limit_bytes=8 * MIB),
    )(spectra, gap_counts.reshape(1, stations))
    group_rows = lax.all_gather(white.astype(jnp.float16), "grp", axis=0, tiled=True).astype(jnp.bfloat16)

    owner = stack_owner.reshape(1, pairs)
    slot = stack_slot.reshape(1, pairs)
    corr, away = pl.pallas_call(
        correlate_kernel,
        out_shape=[
            jax.ShapeDtypeStruct((pairs, LAGS), jnp.bfloat16),
            jax.ShapeDtypeStruct((bins, LAGS), jnp.bfloat16),
        ],
        scratch_shapes=[
            pltpu.VMEM((pairs, group), jnp.bfloat16),
            pltpu.VMEM((pairs, group), jnp.bfloat16),
            pltpu.VMEM((LAGS, 2 * F), jnp.bfloat16),
        ],
        compiler_params=pltpu.CompilerParams(vmem_limit_bytes=24 * MIB),
    )(
        pair_list.T, owner, slot, group_rows, band_weight.reshape(1, F), *tables()
    )
    arrived = lax.ppermute(away, "seg", [(i, i ^ 1) for i in range(seg)])
    kept = pl.pallas_call(
        own_kernel,
        out_shape=jax.ShapeDtypeStruct((bins, LAGS), jnp.float32),
        compiler_params=pltpu.CompilerParams(vmem_limit_bytes=8 * MIB),
        cost_estimate=pl.CostEstimate(flops=2 * bins * pairs * LAGS, bytes_accessed=2 << 20, transcendentals=0),
    )(owner, slot, corr)
    chip = (kept + arrived.astype(jnp.float32)).astype(jnp.bfloat16)
    rows = chip.reshape(CHIPS_X, CHIPS_Y * SLOTS_DEV, LAGS)
    got = lax.all_to_all(
        rows, "seg", split_axis=0, concat_axis=0, tiled=True,
        axis_index_groups=[
            [(y * CHIPS_X + x) * 2 + core for x in range(CHIPS_X)] for y in range(CHIPS_Y) for core in range(2)
        ],
    )
    rows = jnp.sum(got.astype(jnp.float32), axis=0).astype(jnp.bfloat16).reshape(CHIPS_Y, SLOTS_DEV, LAGS)
    got = lax.all_to_all(
        rows, "seg", split_axis=0, concat_axis=0, tiled=True,
        axis_index_groups=[
            [(y * CHIPS_X + x) * 2 + core for y in range(CHIPS_Y)] for x in range(CHIPS_X) for core in range(2)
        ],
    )
    return jnp.sum(got.astype(jnp.float32), axis=0)


def solution(mesh):
    placed = (
        P(("grp", "seg"), None),
        P(("grp", "seg")),
        P(),
        P(("grp", "seg"), None),
        P(("grp", "seg"), None),
        P(("grp", "seg")),
    )
    return jax.shard_map(
        on_device, mesh=mesh, in_specs=placed, out_specs=P(("grp", "seg"), None), check_vma=False
    )
```

```python
import math

import jax
import jax.numpy as jnp
import numpy as np
from jax import lax
from jax.experimental import pallas as pl
from jax.experimental.pallas import tpu as pltpu
from jax.sharding import PartitionSpec as P

F = 2048
LAGS = 256
SAMPLES = 72000
SLOTS_DEV = 32
LIFT = 256.0
FINE = 16
COLUMNS = 256
ROWS = 512
BIN_ROWS = 256
MIB = 1024 * 1024


def tables():
    freqs = np.arange(F, dtype=np.int64)
    coarse = np.arange(0, LAGS, FINE, dtype=np.int64) - LAGS // 2
    fine = np.arange(FINE, dtype=np.int64)
    angles = [(k[:, None] * freqs[None, :]) % (2 * F) * (math.pi / F) for k in (coarse, fine)]
    return [np.concatenate([np.cos(angle), np.sin(angle)]).astype(np.float32) for angle in angles]


def prepare_kernel(
    spectra_hbm, gap_hbm, pairs_hbm, owner_hbm, slot_hbm, weight_hbm, coarse_hbm, fine_hbm,
    white_ref, first_ref, second_ref, bins_ref, table_ref,
    spectra_ref, gap_ref, pairs_ref, owner_ref, slot_ref, weight_ref, coarse_ref, fine_ref, sems,
):
    moved = (
        (weight_hbm, weight_ref), (coarse_hbm, coarse_ref), (fine_hbm, fine_ref), (pairs_hbm, pairs_ref),
        (owner_hbm, owner_ref), (slot_hbm, slot_ref), (gap_hbm, gap_ref), (spectra_hbm, spectra_ref),
    )
    copies = [pltpu.make_async_copy(src, dst, sems.at[i]) for i, (src, dst) in enumerate(moved)]
    for copy in copies:
        copy.start()
    for copy in copies:
        copy.wait()

    weight = weight_ref[...] * (0.25 / math.sqrt(F) / (LIFT * LIFT))
    cos_fine, sin_fine = fine_ref[:FINE, :], fine_ref[FINE:, :]
    count = LAGS // FINE
    for block in range(count):
        cos = weight * coarse_ref[block : block + 1, :]
        sin = weight * coarse_ref[count + block : count + block + 1, :]
        upper = (cos * cos_fine - sin * sin_fine).astype(jnp.bfloat16)
        lower = (-(sin * cos_fine + cos * sin_fine)).astype(jnp.bfloat16)
        rows = slice(block * FINE, block * FINE + FINE)
        for column in range(0, F, COLUMNS):
            here = slice(column, column + COLUMNS)
            table_ref[rows, 2 * column : 2 * column + COLUMNS] = upper[:, here]
            table_ref[rows, 2 * column + COLUMNS : 2 * column + 2 * COLUMNS] = lower[:, here]

    pairs, group = first_ref.shape
    ids = lax.broadcasted_iota(jnp.int32, (group, pairs), 0)
    first_ref[...] = (ids == pairs_ref[0:1, :]).astype(jnp.float32).T.astype(jnp.bfloat16)
    second_ref[...] = (ids == pairs_ref[1:2, :]).astype(jnp.float32).T.astype(jnp.bfloat16)

    core = lax.axis_index("seg") & 1
    owner = owner_ref[...]
    local = (owner >> 1) * SLOTS_DEV + slot_ref[...]
    bins_ref[0:1, :] = jnp.where((owner & 1) == core, -1, local)
    bins_ref[1:2, :] = jnp.where((owner & 1) == core, local, -1)

    stations = spectra_ref.shape[0]
    values = spectra_ref[...].astype(jnp.float32)
    power = jnp.mean(values * values, axis=1, keepdims=True)
    kept = jnp.broadcast_to(SAMPLES - gap_ref[...].astype(jnp.float32), (stations, stations))
    here = lax.broadcasted_iota(jnp.int32, (stations, stations), 0)
    along = lax.broadcasted_iota(jnp.int32, (stations, stations), 1)
    kept = jnp.sum(jnp.where(here == along, kept, 0.0), axis=1, keepdims=True)
    factor = jnp.sqrt(SAMPLES / kept) / jnp.sqrt(power + 1e-06)
    white_ref[...] = (values * factor).astype(jnp.bfloat16) * LIFT


def into_bins(bins, corr_ref, out_ref):
    pairs = corr_ref.shape[0]
    count = out_ref.shape[0]
    for start in range(0, count, BIN_ROWS):
        ids = lax.broadcasted_iota(jnp.int32, (BIN_ROWS, pairs), 0) + start
        place = (ids == bins).astype(jnp.bfloat16)
        out_ref[start : start + BIN_ROWS, :] = jnp.dot(
            place, corr_ref[...], preferred_element_type=jnp.float32
        ).astype(out_ref.dtype)


def correlate_kernel(bins_ref, white_ref, first_ref, second_ref, table_ref, corr_ref, away_ref):
    pairs = corr_ref.shape[0]

    def pick(one_hot, rows):
        return jnp.dot(one_hot, rows, preferred_element_type=jnp.float32)

    def lags(cross, table):
        return lax.dot_general(
            cross, table, (((1,), (1,)), ((), ())), preferred_element_type=jnp.float32
        )

    for start in range(0, pairs, ROWS):
        rows = slice(start, start + ROWS)
        one, two = first_ref[rows, :], second_ref[rows, :]
        total = jnp.zeros((ROWS, LAGS), jnp.float32)
        for column in range(0, F, COLUMNS):
            here = slice(column, column + COLUMNS)
            real = white_ref[:, here]
            imag = white_ref[:, F + column : F + column + COLUMNS]
            real_one, imag_one = pick(one, real), pick(one, imag)
            real_two, imag_two = pick(two, real), pick(two, imag)
            cross = jnp.concatenate(
                [
                    (real_one * real_two + imag_one * imag_two).astype(jnp.bfloat16),
                    (imag_one * real_two - real_one * imag_two).astype(jnp.bfloat16),
                ],
                axis=1,
            )
            total += lags(cross, table_ref[:, 2 * column : 2 * column + 2 * COLUMNS])
        corr_ref[rows, :] = total.astype(jnp.bfloat16)
    into_bins(bins_ref[0:1, :], corr_ref, away_ref)


def own_kernel(bins_ref, corr_ref, out_ref):
    into_bins(bins_ref[1:2, :], corr_ref, out_ref)


def on_device(spectra, gap_counts, band_weight, pair_list, stack_owner, stack_slot):
    stations = spectra.shape[0]
    pairs = pair_list.shape[0]
    seg = lax.axis_size("seg")
    group = stations * lax.axis_size("grp")
    bins = seg // 2 * SLOTS_DEV
    inputs = (
        spectra, gap_counts.reshape(1, stations), pair_list.T, stack_owner.reshape(1, pairs),
        stack_slot.reshape(1, pairs), band_weight.reshape(1, F), *map(jnp.asarray, tables()),
    )
    white, first, second, bin_rows, table = pl.pallas_call(
        prepare_kernel,
        in_specs=[pl.BlockSpec(memory_space=pltpu.HBM)] * len(inputs),
        out_shape=[
            jax.ShapeDtypeStruct(spectra.shape, jnp.bfloat16),
            jax.ShapeDtypeStruct((pairs, group), jnp.bfloat16),
            jax.ShapeDtypeStruct((pairs, group), jnp.bfloat16),
            jax.ShapeDtypeStruct((2, pairs), jnp.int32),
            jax.ShapeDtypeStruct((LAGS, 2 * F), jnp.bfloat16),
        ],
        scratch_shapes=[pltpu.VMEM(x.shape, x.dtype) for x in inputs]
        + [pltpu.SemaphoreType.DMA((len(inputs),))],
        compiler_params=pltpu.CompilerParams(vmem_limit_bytes=16 * MIB),
    )(*[pltpu.with_memory_space_constraint(x, pltpu.HBM) for x in inputs])
    group_rows = lax.all_gather(white.astype(jnp.float16), "grp", axis=0, tiled=True).astype(jnp.bfloat16)

    corr, away = pl.pallas_call(
        correlate_kernel,
        out_shape=[
            jax.ShapeDtypeStruct((pairs, LAGS), jnp.bfloat16),
            jax.ShapeDtypeStruct((bins, LAGS), jnp.bfloat16),
        ],
        compiler_params=pltpu.CompilerParams(vmem_limit_bytes=16 * MIB),
    )(bin_rows, group_rows, first, second, table)
    arrived = lax.ppermute(away, "seg", [(i, i ^ 1) for i in range(seg)])
    kept = pl.pallas_call(
        own_kernel,
        out_shape=jax.ShapeDtypeStruct((bins, LAGS), jnp.float32),
        compiler_params=pltpu.CompilerParams(vmem_limit_bytes=8 * MIB),
        cost_estimate=pl.CostEstimate(flops=2 * bins * pairs * LAGS, bytes_accessed=2 << 20, transcendentals=0),
    )(bin_rows, corr)
    chip = (kept + arrived.astype(jnp.float32)).astype(jnp.bfloat16).reshape(seg // 2, SLOTS_DEV, LAGS)
    got = lax.all_to_all(
        chip, "seg", split_axis=0, concat_axis=0, tiled=True,
        axis_index_groups=[list(range(core, seg, 2)) for core in range(2)],
    )
    return jnp.sum(got.astype(jnp.float32), axis=0)


def solution(mesh):
    placed = (
        P(("grp", "seg"), None),
        P(("grp", "seg")),
        P(),
        P(("grp", "seg"), None),
        P(("grp", "seg"), None),
        P(("grp", "seg")),
    )
    return jax.shard_map(
        on_device, mesh=mesh, in_specs=placed, out_specs=P(("grp", "seg"), None), check_vma=False
    )
```

```python
import math

import jax
import jax.numpy as jnp
import numpy as np
from jax import lax
from jax.experimental import pallas as pl
from jax.experimental.pallas import tpu as pltpu
from jax.sharding import PartitionSpec as P

F = 2048
LAGS = 256
SAMPLES = 72000
SLOTS_DEV = 32
LIFT = 256.0
FINE = 16
SMALL = 6
COLUMNS = 256
ROWS = 512
BIN_ROWS = 128
MIB = 1024 * 1024


def tables():
    freqs = np.arange(F, dtype=np.int64)
    coarse = np.arange(0, LAGS, FINE, dtype=np.int64) - LAGS // 2
    fine = np.arange(FINE, dtype=np.int64)
    angles = [(k[:, None] * freqs[None, :]) % (2 * F) * (math.pi / F) for k in (coarse, fine)]
    return [np.concatenate([np.cos(angle), np.sin(angle)]).astype(np.float32) for angle in angles]


def whiten_kernel(*refs):
    spectra_hbm, gap_hbm, *small_hbm = refs[: 2 + SMALL]
    white_ref, *small_refs = refs[2 + SMALL : 3 + 2 * SMALL]
    spectra_ref, gap_ref, sems = refs[3 + 2 * SMALL :]
    moved = zip((spectra_hbm, gap_hbm, *small_hbm), (spectra_ref, gap_ref, *small_refs))
    copies = [pltpu.make_async_copy(src, dst, sems.at[i]) for i, (src, dst) in enumerate(moved)]
    for copy in copies:
        copy.start()
    for copy in copies[:2]:
        copy.wait()
    stations = spectra_ref.shape[0]
    values = spectra_ref[...].astype(jnp.float32)
    power = jnp.mean(values * values, axis=1, keepdims=True)
    kept = jnp.broadcast_to(SAMPLES - gap_ref[...].astype(jnp.float32), (stations, stations))
    here = lax.broadcasted_iota(jnp.int32, (stations, stations), 0)
    along = lax.broadcasted_iota(jnp.int32, (stations, stations), 1)
    kept = jnp.sum(jnp.where(here == along, kept, 0.0), axis=1, keepdims=True)
    factor = jnp.sqrt(SAMPLES / kept) / jnp.sqrt(power + 1e-06)
    white_ref[...] = (values * factor).astype(jnp.bfloat16) * LIFT
    for copy in copies[2:]:
        copy.wait()


def pick_bins(owner_ref, slot_ref, parity):
    owner = owner_ref[...]
    local = (owner >> 1) * SLOTS_DEV + slot_ref[...]
    return jnp.where((owner & 1) == parity, local, -1)


def into_bins(bins, corr_ref, out_ref):
    pairs = corr_ref.shape[0]
    count = out_ref.shape[0]
    for start in range(0, count, BIN_ROWS):
        ids = lax.broadcasted_iota(jnp.int32, (BIN_ROWS, pairs), 0) + start
        place = (ids == bins).astype(jnp.bfloat16)
        out_ref[start : start + BIN_ROWS, :] = jnp.dot(
            place, corr_ref[...], preferred_element_type=jnp.float32
        ).astype(out_ref.dtype)


def correlate_kernel(
    pairs_ref, owner_ref, slot_ref, white_ref, weight_ref, coarse_ref, fine_ref,
    corr_ref, away_ref, first_ref, second_ref, table_ref,
):
    group = white_ref.shape[0]
    pairs = corr_ref.shape[0]
    ids = lax.broadcasted_iota(jnp.int32, (group, pairs), 0)
    first_ref[...] = (ids == pairs_ref[0:1, :]).astype(jnp.float32).T.astype(jnp.bfloat16)
    second_ref[...] = (ids == pairs_ref[1:2, :]).astype(jnp.float32).T.astype(jnp.bfloat16)
    weight = weight_ref[...] * (0.25 / math.sqrt(F) / (LIFT * LIFT))
    cos_fine, sin_fine = fine_ref[:FINE, :], fine_ref[FINE:, :]
    blocks = LAGS // FINE
    for block in range(blocks):
        cos = weight * coarse_ref[block : block + 1, :]
        sin = weight * coarse_ref[blocks + block : blocks + block + 1, :]
        upper = (cos * cos_fine - sin * sin_fine).astype(jnp.bfloat16)
        lower = (-(sin * cos_fine + cos * sin_fine)).astype(jnp.bfloat16)
        rows = slice(block * FINE, block * FINE + FINE)
        for column in range(0, F, COLUMNS):
            here = slice(column, column + COLUMNS)
            table_ref[rows, 2 * column : 2 * column + COLUMNS] = upper[:, here]
            table_ref[rows, 2 * column + COLUMNS : 2 * column + 2 * COLUMNS] = lower[:, here]

    def pick(one_hot, rows):
        return jnp.dot(one_hot, rows, preferred_element_type=jnp.float32)

    def lags(cross, table):
        return lax.dot_general(
            cross, table, (((1,), (1,)), ((), ())), preferred_element_type=jnp.float32
        )

    for start in range(0, pairs, ROWS):
        rows = slice(start, start + ROWS)
        one, two = first_ref[rows, :], second_ref[rows, :]
        total = jnp.zeros((ROWS, LAGS), jnp.float32)
        for column in range(0, F, COLUMNS):
            here = slice(column, column + COLUMNS)
            real = white_ref[:, here]
            imag = white_ref[:, F + column : F + column + COLUMNS]
            real_one, imag_one = pick(one, real), pick(one, imag)
            real_two, imag_two = pick(two, real), pick(two, imag)
            cross = jnp.concatenate(
                [
                    (real_one * real_two + imag_one * imag_two).astype(jnp.bfloat16),
                    (imag_one * real_two - real_one * imag_two).astype(jnp.bfloat16),
                ],
                axis=1,
            )
            total += lags(cross, table_ref[:, 2 * column : 2 * column + 2 * COLUMNS])
        corr_ref[rows, :] = total.astype(jnp.bfloat16)
    core = lax.axis_index("seg") & 1
    into_bins(pick_bins(owner_ref, slot_ref, 1 - core), corr_ref, away_ref)


def own_kernel(owner_ref, slot_ref, corr_ref, out_ref):
    core = lax.axis_index("seg") & 1
    into_bins(pick_bins(owner_ref, slot_ref, core), corr_ref, out_ref)


def on_device(spectra, gap_counts, band_weight, pair_list, stack_owner, stack_slot):
    stations = spectra.shape[0]
    pairs = pair_list.shape[0]
    seg = lax.axis_size("seg")
    group = stations * lax.axis_size("grp")
    bins = seg // 2 * SLOTS_DEV
    inputs = (
        spectra, gap_counts.reshape(1, stations), pair_list.T, stack_owner.reshape(1, pairs),
        stack_slot.reshape(1, pairs), band_weight.reshape(1, F), *map(jnp.asarray, tables()),
    )
    white, ends, owner, slot, weight, coarse, fine = pl.pallas_call(
        whiten_kernel,
        in_specs=[pl.BlockSpec(memory_space=pltpu.HBM)] * len(inputs),
        out_shape=[jax.ShapeDtypeStruct(spectra.shape, jnp.bfloat16)]
        + [jax.ShapeDtypeStruct(x.shape, x.dtype) for x in inputs[2:]],
        scratch_shapes=[
            pltpu.VMEM(inputs[0].shape, inputs[0].dtype),
            pltpu.VMEM(inputs[1].shape, inputs[1].dtype),
            pltpu.SemaphoreType.DMA((len(inputs),)),
        ],
        compiler_params=pltpu.CompilerParams(vmem_limit_bytes=8 * MIB),
    )(*[pltpu.with_memory_space_constraint(x, pltpu.HBM) for x in inputs])
    group_rows = lax.all_gather(white.astype(jnp.float16), "grp", axis=0, tiled=True).astype(jnp.bfloat16)

    corr, away = pl.pallas_call(
        correlate_kernel,
        out_shape=[
            jax.ShapeDtypeStruct((pairs, LAGS), jnp.bfloat16),
            jax.ShapeDtypeStruct((bins, LAGS), jnp.bfloat16),
        ],
        scratch_shapes=[
            pltpu.VMEM((pairs, group), jnp.bfloat16),
            pltpu.VMEM((pairs, group), jnp.bfloat16),
            pltpu.VMEM((LAGS, 2 * F), jnp.bfloat16),
        ],
        compiler_params=pltpu.CompilerParams(vmem_limit_bytes=24 * MIB),
    )(
        ends, owner, slot, group_rows, weight, coarse, fine
    )
    arrived = lax.ppermute(away, "seg", [(i, i ^ 1) for i in range(seg)])
    kept = pl.pallas_call(
        own_kernel,
        out_shape=jax.ShapeDtypeStruct((bins, LAGS), jnp.float32),
        compiler_params=pltpu.CompilerParams(vmem_limit_bytes=8 * MIB),
        cost_estimate=pl.CostEstimate(flops=2 * bins * pairs * LAGS, bytes_accessed=2 << 20, transcendentals=0),
    )(owner, slot, corr)
    chip = (kept + arrived.astype(jnp.float32)).astype(jnp.bfloat16).reshape(seg // 2, SLOTS_DEV, LAGS)
    got = lax.all_to_all(
        chip, "seg", split_axis=0, concat_axis=0, tiled=True,
        axis_index_groups=[list(range(core, seg, 2)) for core in range(2)],
    )
    return jnp.sum(got.astype(jnp.float32), axis=0)


def solution(mesh):
    placed = (
        P(("grp", "seg"), None),
        P(("grp", "seg")),
        P(),
        P(("grp", "seg"), None),
        P(("grp", "seg"), None),
        P(("grp", "seg")),
    )
    return jax.shard_map(
        on_device, mesh=mesh, in_specs=placed, out_specs=P(("grp", "seg"), None), check_vma=False
    )
```

```python
import math

import jax
import jax.numpy as jnp
import numpy as np
from jax import lax
from jax.experimental import pallas as pl
from jax.experimental.pallas import tpu as pltpu
from jax.sharding import PartitionSpec as P

F = 2048
LAGS = 256
SAMPLES = 72000
SLOTS_DEV = 32
CHIPS_Y, CHIPS_X = 8, 4
LIFT = 256.0
FINE = 16
SMALL = 6
COLUMNS = 256
ROWS = 512
BIN_ROWS = 128
MIB = 1024 * 1024


def tables():
    freqs = np.arange(F, dtype=np.int64)
    coarse = np.arange(0, LAGS, FINE, dtype=np.int64) - LAGS // 2
    fine = np.arange(FINE, dtype=np.int64)
    angles = [(k[:, None] * freqs[None, :]) % (2 * F) * (math.pi / F) for k in (coarse, fine)]
    return [np.concatenate([np.cos(angle), np.sin(angle)]).astype(np.float32) for angle in angles]


def whiten_kernel(*refs):
    spectra_hbm, gap_hbm, *small_hbm = refs[: 2 + SMALL]
    white_ref, *small_refs = refs[2 + SMALL : 3 + 2 * SMALL]
    spectra_ref, gap_ref, sems = refs[3 + 2 * SMALL :]
    moved = zip((spectra_hbm, gap_hbm, *small_hbm), (spectra_ref, gap_ref, *small_refs))
    copies = [pltpu.make_async_copy(src, dst, sems.at[i]) for i, (src, dst) in enumerate(moved)]
    for copy in copies:
        copy.start()
    for copy in copies[:2]:
        copy.wait()
    stations = spectra_ref.shape[0]
    values = spectra_ref[...].astype(jnp.float32)
    power = jnp.mean(values * values, axis=1, keepdims=True)
    kept = jnp.broadcast_to(SAMPLES - gap_ref[...].astype(jnp.float32), (stations, stations))
    here = lax.broadcasted_iota(jnp.int32, (stations, stations), 0)
    along = lax.broadcasted_iota(jnp.int32, (stations, stations), 1)
    kept = jnp.sum(jnp.where(here == along, kept, 0.0), axis=1, keepdims=True)
    factor = jnp.sqrt(SAMPLES / kept) / jnp.sqrt(power + 1e-06)
    white_ref[...] = (values * factor).astype(jnp.bfloat16) * LIFT
    for copy in copies[2:]:
        copy.wait()


def far_first():
    halves = [[k for i in range(n // 2) for k in (i, i + n // 2)] for n in (CHIPS_Y, CHIPS_X)]
    return [y * CHIPS_X + x for y in halves[0] for x in halves[1]]


def pick_bins(owner_ref, slot_ref, parity):
    owner = owner_ref[...]
    y, x = owner // (2 * CHIPS_X), owner // 2 % CHIPS_X
    place = (2 * (y % (CHIPS_Y // 2)) + y // (CHIPS_Y // 2)) * CHIPS_X + 2 * (x % 2) + x // 2
    local = place * SLOTS_DEV + slot_ref[...]
    return jnp.where((owner & 1) == parity, local, -1)


def into_bins(bins, corr_ref, out_ref):
    pairs = corr_ref.shape[0]
    count = out_ref.shape[0]
    for start in range(0, count, BIN_ROWS):
        ids = lax.broadcasted_iota(jnp.int32, (BIN_ROWS, pairs), 0) + start
        place = (ids == bins).astype(jnp.bfloat16)
        out_ref[start : start + BIN_ROWS, :] = jnp.dot(
            place, corr_ref[...], preferred_element_type=jnp.float32
        ).astype(out_ref.dtype)


def correlate_kernel(
    pairs_ref, owner_ref, slot_ref, white_ref, weight_ref, coarse_ref, fine_ref,
    corr_ref, away_ref, first_ref, second_ref, table_ref,
):
    group = white_ref.shape[0]
    pairs = corr_ref.shape[0]
    ids = lax.broadcasted_iota(jnp.int32, (group, pairs), 0)
    first_ref[...] = (ids == pairs_ref[0:1, :]).astype(jnp.float32).T.astype(jnp.bfloat16)
    second_ref[...] = (ids == pairs_ref[1:2, :]).astype(jnp.float32).T.astype(jnp.bfloat16)
    weight = weight_ref[...] * (0.25 / math.sqrt(F) / (LIFT * LIFT))
    cos_fine, sin_fine = fine_ref[:FINE, :], fine_ref[FINE:, :]
    blocks = LAGS // FINE
    for block in range(blocks):
        cos = weight * coarse_ref[block : block + 1, :]
        sin = weight * coarse_ref[blocks + block : blocks + block + 1, :]
        upper = (cos * cos_fine - sin * sin_fine).astype(jnp.bfloat16)
        lower = (-(sin * cos_fine + cos * sin_fine)).astype(jnp.bfloat16)
        rows = slice(block * FINE, block * FINE + FINE)
        for column in range(0, F, COLUMNS):
            here = slice(column, column + COLUMNS)
            table_ref[rows, 2 * column : 2 * column + COLUMNS] = upper[:, here]
            table_ref[rows, 2 * column + COLUMNS : 2 * column + 2 * COLUMNS] = lower[:, here]

    def pick(one_hot, rows):
        return jnp.dot(one_hot, rows, preferred_element_type=jnp.float32)

    def lags(cross, table):
        return lax.dot_general(
            cross, table, (((1,), (1,)), ((), ())), preferred_element_type=jnp.float32
        )

    for start in range(0, pairs, ROWS):
        rows = slice(start, start + ROWS)
        one, two = first_ref[rows, :], second_ref[rows, :]
        total = jnp.zeros((ROWS, LAGS), jnp.float32)
        for column in range(0, F, COLUMNS):
            here = slice(column, column + COLUMNS)
            real = white_ref[:, here]
            imag = white_ref[:, F + column : F + column + COLUMNS]
            real_one, imag_one = pick(one, real), pick(one, imag)
            real_two, imag_two = pick(two, real), pick(two, imag)
            cross = jnp.concatenate(
                [
                    (real_one * real_two + imag_one * imag_two).astype(jnp.bfloat16),
                    (imag_one * real_two - real_one * imag_two).astype(jnp.bfloat16),
                ],
                axis=1,
            )
            total += lags(cross, table_ref[:, 2 * column : 2 * column + 2 * COLUMNS])
        corr_ref[rows, :] = total.astype(jnp.bfloat16)
    core = lax.axis_index("seg") & 1
    into_bins(pick_bins(owner_ref, slot_ref, 1 - core), corr_ref, away_ref)


def own_kernel(owner_ref, slot_ref, corr_ref, out_ref):
    core = lax.axis_index("seg") & 1
    into_bins(pick_bins(owner_ref, slot_ref, core), corr_ref, out_ref)


def on_device(spectra, gap_counts, band_weight, pair_list, stack_owner, stack_slot):
    stations = spectra.shape[0]
    pairs = pair_list.shape[0]
    seg = lax.axis_size("seg")
    group = stations * lax.axis_size("grp")
    bins = seg // 2 * SLOTS_DEV
    inputs = (
        spectra, gap_counts.reshape(1, stations), pair_list.T, stack_owner.reshape(1, pairs),
        stack_slot.reshape(1, pairs), band_weight.reshape(1, F), *map(jnp.asarray, tables()),
    )
    white, ends, owner, slot, weight, coarse, fine = pl.pallas_call(
        whiten_kernel,
        in_specs=[pl.BlockSpec(memory_space=pltpu.HBM)] * len(inputs),
        out_shape=[jax.ShapeDtypeStruct(spectra.shape, jnp.bfloat16)]
        + [jax.ShapeDtypeStruct(x.shape, x.dtype) for x in inputs[2:]],
        scratch_shapes=[
            pltpu.VMEM(inputs[0].shape, inputs[0].dtype),
            pltpu.VMEM(inputs[1].shape, inputs[1].dtype),
            pltpu.SemaphoreType.DMA((len(inputs),)),
        ],
        compiler_params=pltpu.CompilerParams(vmem_limit_bytes=8 * MIB),
    )(*[pltpu.with_memory_space_constraint(x, pltpu.HBM) for x in inputs])
    group_rows = lax.all_gather(white.astype(jnp.float16), "grp", axis=0, tiled=True).astype(jnp.bfloat16)

    corr, away = pl.pallas_call(
        correlate_kernel,
        out_shape=[
            jax.ShapeDtypeStruct((pairs, LAGS), jnp.bfloat16),
            jax.ShapeDtypeStruct((bins, LAGS), jnp.bfloat16),
        ],
        scratch_shapes=[
            pltpu.VMEM((pairs, group), jnp.bfloat16),
            pltpu.VMEM((pairs, group), jnp.bfloat16),
            pltpu.VMEM((LAGS, 2 * F), jnp.bfloat16),
        ],
        compiler_params=pltpu.CompilerParams(vmem_limit_bytes=24 * MIB),
    )(
        ends, owner, slot, group_rows, weight, coarse, fine
    )
    arrived = lax.ppermute(away, "seg", [(i, i ^ 1) for i in range(seg)])
    kept = pl.pallas_call(
        own_kernel,
        out_shape=jax.ShapeDtypeStruct((bins, LAGS), jnp.float32),
        compiler_params=pltpu.CompilerParams(vmem_limit_bytes=8 * MIB),
        cost_estimate=pl.CostEstimate(flops=2 * bins * pairs * LAGS, bytes_accessed=2 << 20, transcendentals=0),
    )(owner, slot, corr)
    chip = (kept + arrived.astype(jnp.float32)).astype(jnp.bfloat16).reshape(seg // 2, SLOTS_DEV, LAGS)
    got = lax.all_to_all(
        chip, "seg", split_axis=0, concat_axis=0, tiled=True,
        axis_index_groups=[[2 * chip + core for chip in far_first()] for core in range(2)],
    )
    return jnp.sum(got.astype(jnp.float32), axis=0)


def solution(mesh):
    placed = (
        P(("grp", "seg"), None),
        P(("grp", "seg")),
        P(),
        P(("grp", "seg"), None),
        P(("grp", "seg"), None),
        P(("grp", "seg")),
    )
    return jax.shard_map(
        on_device, mesh=mesh, in_specs=placed, out_specs=P(("grp", "seg"), None), check_vma=False
    )
```

```python
import math

import jax
import jax.numpy as jnp
import numpy as np
from jax import lax
from jax.experimental import pallas as pl
from jax.experimental.pallas import tpu as pltpu
from jax.sharding import PartitionSpec as P

F = 2048
LAGS = 256
SAMPLES = 72000
SLOTS_DEV = 32
CHIPS = 32
LIFT = 256.0
FINE = 16
SMALL = 6
COLUMNS = 256
ROWS = 512
BIN_ROWS = 128
MIB = 1024 * 1024


def tables():
    freqs = np.arange(F, dtype=np.int64)
    coarse = np.arange(0, LAGS, FINE, dtype=np.int64) - LAGS // 2
    fine = np.arange(FINE, dtype=np.int64)
    angles = [(k[:, None] * freqs[None, :]) % (2 * F) * (math.pi / F) for k in (coarse, fine)]
    return [np.concatenate([np.cos(angle), np.sin(angle)]).astype(np.float32) for angle in angles]


def whiten_kernel(*refs):
    spectra_hbm, gap_hbm, *small_hbm = refs[: 2 + SMALL]
    white_ref, *small_refs = refs[2 + SMALL : 3 + 2 * SMALL]
    spectra_ref, gap_ref, sems = refs[3 + 2 * SMALL :]
    moved = zip((spectra_hbm, gap_hbm, *small_hbm), (spectra_ref, gap_ref, *small_refs))
    copies = [pltpu.make_async_copy(src, dst, sems.at[i]) for i, (src, dst) in enumerate(moved)]
    for copy in copies:
        copy.start()
    for copy in copies[:2]:
        copy.wait()
    stations = spectra_ref.shape[0]
    values = spectra_ref[...].astype(jnp.float32)
    power = jnp.mean(values * values, axis=1, keepdims=True)
    kept = jnp.broadcast_to(SAMPLES - gap_ref[...].astype(jnp.float32), (stations, stations))
    here = lax.broadcasted_iota(jnp.int32, (stations, stations), 0)
    along = lax.broadcasted_iota(jnp.int32, (stations, stations), 1)
    kept = jnp.sum(jnp.where(here == along, kept, 0.0), axis=1, keepdims=True)
    factor = jnp.sqrt(SAMPLES / kept) / jnp.sqrt(power + 1e-06)
    white_ref[...] = (values * factor).astype(jnp.bfloat16) * LIFT
    for copy in copies[2:]:
        copy.wait()


def pick_bins(owner_ref, slot_ref, parity):
    owner = owner_ref[...]
    local = (CHIPS - 1 - (owner >> 1)) * SLOTS_DEV + slot_ref[...]
    return jnp.where((owner & 1) == parity, local, -1)


def into_bins(bins, corr_ref, out_ref):
    pairs = corr_ref.shape[0]
    count = out_ref.shape[0]
    for start in range(0, count, BIN_ROWS):
        ids = lax.broadcasted_iota(jnp.int32, (BIN_ROWS, pairs), 0) + start
        place = (ids == bins).astype(jnp.bfloat16)
        out_ref[start : start + BIN_ROWS, :] = jnp.dot(
            place, corr_ref[...], preferred_element_type=jnp.float32
        ).astype(out_ref.dtype)


def correlate_kernel(
    pairs_ref, owner_ref, slot_ref, white_ref, weight_ref, coarse_ref, fine_ref,
    corr_ref, away_ref, first_ref, second_ref, table_ref,
):
    group = white_ref.shape[0]
    pairs = corr_ref.shape[0]
    ids = lax.broadcasted_iota(jnp.int32, (group, pairs), 0)
    first_ref[...] = (ids == pairs_ref[0:1, :]).astype(jnp.float32).T.astype(jnp.bfloat16)
    second_ref[...] = (ids == pairs_ref[1:2, :]).astype(jnp.float32).T.astype(jnp.bfloat16)
    weight = weight_ref[...] * (0.25 / math.sqrt(F) / (LIFT * LIFT))
    cos_fine, sin_fine = fine_ref[:FINE, :], fine_ref[FINE:, :]
    blocks = LAGS // FINE
    for block in range(blocks):
        cos = weight * coarse_ref[block : block + 1, :]
        sin = weight * coarse_ref[blocks + block : blocks + block + 1, :]
        upper = (cos * cos_fine - sin * sin_fine).astype(jnp.bfloat16)
        lower = (-(sin * cos_fine + cos * sin_fine)).astype(jnp.bfloat16)
        rows = slice(block * FINE, block * FINE + FINE)
        for column in range(0, F, COLUMNS):
            here = slice(column, column + COLUMNS)
            table_ref[rows, 2 * column : 2 * column + COLUMNS] = upper[:, here]
            table_ref[rows, 2 * column + COLUMNS : 2 * column + 2 * COLUMNS] = lower[:, here]

    def pick(one_hot, rows):
        return jnp.dot(one_hot, rows, preferred_element_type=jnp.float32)

    def lags(cross, table):
        return lax.dot_general(
            cross, table, (((1,), (1,)), ((), ())), preferred_element_type=jnp.float32
        )

    for start in range(0, pairs, ROWS):
        rows = slice(start, start + ROWS)
        one, two = first_ref[rows, :], second_ref[rows, :]
        total = jnp.zeros((ROWS, LAGS), jnp.float32)
        for column in range(0, F, COLUMNS):
            here = slice(column, column + COLUMNS)
            real = white_ref[:, here]
            imag = white_ref[:, F + column : F + column + COLUMNS]
            real_one, imag_one = pick(one, real), pick(one, imag)
            real_two, imag_two = pick(two, real), pick(two, imag)
            cross = jnp.concatenate(
                [
                    (real_one * real_two + imag_one * imag_two).astype(jnp.bfloat16),
                    (imag_one * real_two - real_one * imag_two).astype(jnp.bfloat16),
                ],
                axis=1,
            )
            total += lags(cross, table_ref[:, 2 * column : 2 * column + 2 * COLUMNS])
        corr_ref[rows, :] = total.astype(jnp.bfloat16)
    core = lax.axis_index("seg") & 1
    into_bins(pick_bins(owner_ref, slot_ref, 1 - core), corr_ref, away_ref)


def own_kernel(owner_ref, slot_ref, corr_ref, out_ref):
    core = lax.axis_index("seg") & 1
    into_bins(pick_bins(owner_ref, slot_ref, core), corr_ref, out_ref)


def on_device(spectra, gap_counts, band_weight, pair_list, stack_owner, stack_slot):
    stations = spectra.shape[0]
    pairs = pair_list.shape[0]
    seg = lax.axis_size("seg")
    group = stations * lax.axis_size("grp")
    bins = seg // 2 * SLOTS_DEV
    inputs = (
        spectra, gap_counts.reshape(1, stations), pair_list.T, stack_owner.reshape(1, pairs),
        stack_slot.reshape(1, pairs), band_weight.reshape(1, F), *map(jnp.asarray, tables()),
    )
    white, ends, owner, slot, weight, coarse, fine = pl.pallas_call(
        whiten_kernel,
        in_specs=[pl.BlockSpec(memory_space=pltpu.HBM)] * len(inputs),
        out_shape=[jax.ShapeDtypeStruct(spectra.shape, jnp.bfloat16)]
        + [jax.ShapeDtypeStruct(x.shape, x.dtype) for x in inputs[2:]],
        scratch_shapes=[
            pltpu.VMEM(inputs[0].shape, inputs[0].dtype),
            pltpu.VMEM(inputs[1].shape, inputs[1].dtype),
            pltpu.SemaphoreType.DMA((len(inputs),)),
        ],
        compiler_params=pltpu.CompilerParams(vmem_limit_bytes=8 * MIB),
    )(*[pltpu.with_memory_space_constraint(x, pltpu.HBM) for x in inputs])
    group_rows = lax.all_gather(white.astype(jnp.float16), "grp", axis=0, tiled=True).astype(jnp.bfloat16)

    corr, away = pl.pallas_call(
        correlate_kernel,
        out_shape=[
            jax.ShapeDtypeStruct((pairs, LAGS), jnp.bfloat16),
            jax.ShapeDtypeStruct((bins, LAGS), jnp.bfloat16),
        ],
        scratch_shapes=[
            pltpu.VMEM((pairs, group), jnp.bfloat16),
            pltpu.VMEM((pairs, group), jnp.bfloat16),
            pltpu.VMEM((LAGS, 2 * F), jnp.bfloat16),
        ],
        compiler_params=pltpu.CompilerParams(vmem_limit_bytes=24 * MIB),
    )(
        ends, owner, slot, group_rows, weight, coarse, fine
    )
    arrived = lax.ppermute(away, "seg", [(i, i ^ 1) for i in range(seg)])
    kept = pl.pallas_call(
        own_kernel,
        out_shape=jax.ShapeDtypeStruct((bins, LAGS), jnp.float32),
        compiler_params=pltpu.CompilerParams(vmem_limit_bytes=8 * MIB),
        cost_estimate=pl.CostEstimate(flops=2 * bins * pairs * LAGS, bytes_accessed=2 << 20, transcendentals=0),
    )(owner, slot, corr)
    chip = (kept + arrived.astype(jnp.float32)).astype(jnp.bfloat16).reshape(seg // 2, SLOTS_DEV, LAGS)
    got = lax.all_to_all(
        chip, "seg", split_axis=0, concat_axis=0, tiled=True,
        axis_index_groups=[list(range(core, seg, 2))[::-1] for core in range(2)],
    )
    return jnp.sum(got.astype(jnp.float32), axis=0)


def solution(mesh):
    placed = (
        P(("grp", "seg"), None),
        P(("grp", "seg")),
        P(),
        P(("grp", "seg"), None),
        P(("grp", "seg"), None),
        P(("grp", "seg")),
    )
    return jax.shard_map(
        on_device, mesh=mesh, in_specs=placed, out_specs=P(("grp", "seg"), None), check_vma=False
    )
```

```python
import math

import jax
import jax.numpy as jnp
import numpy as np
from jax import lax
from jax.experimental import pallas as pl
from jax.experimental.pallas import tpu as pltpu
from jax.sharding import PartitionSpec as P

F = 2048
LAGS = 256
SAMPLES = 72000
SLOTS_DEV = 32
ORDER = (
    18, 19, 22, 23, 30, 31, 17, 21, 29, 26, 27, 16, 20, 28, 25, 14,
    15, 10, 11, 13, 9, 24, 12, 6, 7, 8, 5, 2, 3, 1, 4, 0,
)
LIFT = 256.0
FINE = 16
SMALL = 6
COLUMNS = 256
ROWS = 512
BIN_ROWS = 128
MIB = 1024 * 1024


def tables():
    freqs = np.arange(F, dtype=np.int64)
    coarse = np.arange(0, LAGS, FINE, dtype=np.int64) - LAGS // 2
    fine = np.arange(FINE, dtype=np.int64)
    angles = [(k[:, None] * freqs[None, :]) % (2 * F) * (math.pi / F) for k in (coarse, fine)]
    return [np.concatenate([np.cos(angle), np.sin(angle)]).astype(np.float32) for angle in angles]


def whiten_kernel(*refs):
    spectra_hbm, gap_hbm, *small_hbm = refs[: 2 + SMALL]
    white_ref, *small_refs = refs[2 + SMALL : 3 + 2 * SMALL]
    spectra_ref, gap_ref, sems = refs[3 + 2 * SMALL :]
    moved = zip((spectra_hbm, gap_hbm, *small_hbm), (spectra_ref, gap_ref, *small_refs))
    copies = [pltpu.make_async_copy(src, dst, sems.at[i]) for i, (src, dst) in enumerate(moved)]
    for copy in copies:
        copy.start()
    for copy in copies[:2]:
        copy.wait()
    stations = spectra_ref.shape[0]
    values = spectra_ref[...].astype(jnp.float32)
    power = jnp.mean(values * values, axis=1, keepdims=True)
    kept = jnp.broadcast_to(SAMPLES - gap_ref[...].astype(jnp.float32), (stations, stations))
    here = lax.broadcasted_iota(jnp.int32, (stations, stations), 0)
    along = lax.broadcasted_iota(jnp.int32, (stations, stations), 1)
    kept = jnp.sum(jnp.where(here == along, kept, 0.0), axis=1, keepdims=True)
    factor = jnp.sqrt(SAMPLES / kept) / jnp.sqrt(power + 1e-06)
    white_ref[...] = (values * factor).astype(jnp.bfloat16) * LIFT
    for copy in copies[2:]:
        copy.wait()


def pick_bins(owner_ref, slot_ref, parity):
    owner = owner_ref[...]
    chip = owner >> 1
    place = jnp.zeros_like(chip)
    for position, number in enumerate(ORDER):
        place = jnp.where(chip == number, position, place)
    local = place * SLOTS_DEV + slot_ref[...]
    return jnp.where((owner & 1) == parity, local, -1)


def into_bins(bins, corr_ref, out_ref):
    pairs = corr_ref.shape[0]
    count = out_ref.shape[0]
    for start in range(0, count, BIN_ROWS):
        ids = lax.broadcasted_iota(jnp.int32, (BIN_ROWS, pairs), 0) + start
        place = (ids == bins).astype(jnp.bfloat16)
        out_ref[start : start + BIN_ROWS, :] = jnp.dot(
            place, corr_ref[...], preferred_element_type=jnp.float32
        ).astype(out_ref.dtype)


def correlate_kernel(
    pairs_ref, owner_ref, slot_ref, white_ref, weight_ref, coarse_ref, fine_ref,
    corr_ref, away_ref, first_ref, second_ref, table_ref,
):
    group = white_ref.shape[0]
    pairs = corr_ref.shape[0]
    ids = lax.broadcasted_iota(jnp.int32, (group, pairs), 0)
    first_ref[...] = (ids == pairs_ref[0:1, :]).astype(jnp.float32).T.astype(jnp.bfloat16)
    second_ref[...] = (ids == pairs_ref[1:2, :]).astype(jnp.float32).T.astype(jnp.bfloat16)
    weight = weight_ref[...] * (0.25 / math.sqrt(F) / (LIFT * LIFT))
    cos_fine, sin_fine = fine_ref[:FINE, :], fine_ref[FINE:, :]
    blocks = LAGS // FINE
    for block in range(blocks):
        cos = weight * coarse_ref[block : block + 1, :]
        sin = weight * coarse_ref[blocks + block : blocks + block + 1, :]
        upper = (cos * cos_fine - sin * sin_fine).astype(jnp.bfloat16)
        lower = (-(sin * cos_fine + cos * sin_fine)).astype(jnp.bfloat16)
        rows = slice(block * FINE, block * FINE + FINE)
        for column in range(0, F, COLUMNS):
            here = slice(column, column + COLUMNS)
            table_ref[rows, 2 * column : 2 * column + COLUMNS] = upper[:, here]
            table_ref[rows, 2 * column + COLUMNS : 2 * column + 2 * COLUMNS] = lower[:, here]

    def pick(one_hot, rows):
        return jnp.dot(one_hot, rows, preferred_element_type=jnp.float32)

    def lags(cross, table):
        return lax.dot_general(
            cross, table, (((1,), (1,)), ((), ())), preferred_element_type=jnp.float32
        )

    for start in range(0, pairs, ROWS):
        rows = slice(start, start + ROWS)
        one, two = first_ref[rows, :], second_ref[rows, :]
        total = jnp.zeros((ROWS, LAGS), jnp.float32)
        for column in range(0, F, COLUMNS):
            here = slice(column, column + COLUMNS)
            real = white_ref[:, here]
            imag = white_ref[:, F + column : F + column + COLUMNS]
            real_one, imag_one = pick(one, real), pick(one, imag)
            real_two, imag_two = pick(two, real), pick(two, imag)
            cross = jnp.concatenate(
                [
                    (real_one * real_two + imag_one * imag_two).astype(jnp.bfloat16),
                    (imag_one * real_two - real_one * imag_two).astype(jnp.bfloat16),
                ],
                axis=1,
            )
            total += lags(cross, table_ref[:, 2 * column : 2 * column + 2 * COLUMNS])
        corr_ref[rows, :] = total.astype(jnp.bfloat16)
    core = lax.axis_index("seg") & 1
    into_bins(pick_bins(owner_ref, slot_ref, 1 - core), corr_ref, away_ref)


def own_kernel(owner_ref, slot_ref, corr_ref, out_ref):
    core = lax.axis_index("seg") & 1
    into_bins(pick_bins(owner_ref, slot_ref, core), corr_ref, out_ref)


def on_device(spectra, gap_counts, band_weight, pair_list, stack_owner, stack_slot):
    stations = spectra.shape[0]
    pairs = pair_list.shape[0]
    seg = lax.axis_size("seg")
    group = stations * lax.axis_size("grp")
    bins = seg // 2 * SLOTS_DEV
    inputs = (
        spectra, gap_counts.reshape(1, stations), pair_list.T, stack_owner.reshape(1, pairs),
        stack_slot.reshape(1, pairs), band_weight.reshape(1, F), *map(jnp.asarray, tables()),
    )
    white, ends, owner, slot, weight, coarse, fine = pl.pallas_call(
        whiten_kernel,
        in_specs=[pl.BlockSpec(memory_space=pltpu.HBM)] * len(inputs),
        out_shape=[jax.ShapeDtypeStruct(spectra.shape, jnp.bfloat16)]
        + [jax.ShapeDtypeStruct(x.shape, x.dtype) for x in inputs[2:]],
        scratch_shapes=[
            pltpu.VMEM(inputs[0].shape, inputs[0].dtype),
            pltpu.VMEM(inputs[1].shape, inputs[1].dtype),
            pltpu.SemaphoreType.DMA((len(inputs),)),
        ],
        compiler_params=pltpu.CompilerParams(vmem_limit_bytes=8 * MIB),
    )(*[pltpu.with_memory_space_constraint(x, pltpu.HBM) for x in inputs])
    group_rows = lax.all_gather(white.astype(jnp.float16), "grp", axis=0, tiled=True).astype(jnp.bfloat16)

    corr, away = pl.pallas_call(
        correlate_kernel,
        out_shape=[
            jax.ShapeDtypeStruct((pairs, LAGS), jnp.bfloat16),
            jax.ShapeDtypeStruct((bins, LAGS), jnp.bfloat16),
        ],
        scratch_shapes=[
            pltpu.VMEM((pairs, group), jnp.bfloat16),
            pltpu.VMEM((pairs, group), jnp.bfloat16),
            pltpu.VMEM((LAGS, 2 * F), jnp.bfloat16),
        ],
        compiler_params=pltpu.CompilerParams(vmem_limit_bytes=24 * MIB),
    )(
        ends, owner, slot, group_rows, weight, coarse, fine
    )
    arrived = lax.ppermute(away, "seg", [(i, i ^ 1) for i in range(seg)])
    kept = pl.pallas_call(
        own_kernel,
        out_shape=jax.ShapeDtypeStruct((bins, LAGS), jnp.float32),
        compiler_params=pltpu.CompilerParams(vmem_limit_bytes=8 * MIB),
        cost_estimate=pl.CostEstimate(flops=2 * bins * pairs * LAGS, bytes_accessed=2 << 20, transcendentals=0),
    )(owner, slot, corr)
    chip = (kept + arrived.astype(jnp.float32)).astype(jnp.bfloat16).reshape(seg // 2, SLOTS_DEV, LAGS)
    got = lax.all_to_all(
        chip, "seg", split_axis=0, concat_axis=0, tiled=True,
        axis_index_groups=[[2 * chip + core for chip in ORDER] for core in range(2)],
    )
    return jnp.sum(got.astype(jnp.float32), axis=0)


def solution(mesh):
    placed = (
        P(("grp", "seg"), None),
        P(("grp", "seg")),
        P(),
        P(("grp", "seg"), None),
        P(("grp", "seg"), None),
        P(("grp", "seg")),
    )
    return jax.shard_map(
        on_device, mesh=mesh, in_specs=placed, out_specs=P(("grp", "seg"), None), check_vma=False
    )
```

```python
import math

import jax
import jax.numpy as jnp
import numpy as np
from jax import lax
from jax.experimental import pallas as pl
from jax.experimental.pallas import tpu as pltpu
from jax.sharding import PartitionSpec as P

F = 2048
LAGS = 256
SAMPLES = 72000
SLOTS_DEV = 32
ORDER = (
    18, 19, 22, 23, 30, 31, 17, 21, 29, 26, 27, 16, 20, 28, 25, 14,
    15, 10, 11, 13, 9, 24, 12, 6, 7, 8, 5, 2, 3, 1, 4, 0,
)
LIFT = 256.0
FINE = 16
SMALL = 6
COLUMNS = 256
ROWS = 512
BIN_ROWS = 128
MIB = 1024 * 1024


def tables():
    freqs = np.arange(F, dtype=np.int64)
    coarse = np.arange(0, LAGS, FINE, dtype=np.int64) - LAGS // 2
    fine = np.arange(FINE, dtype=np.int64)
    angles = [(k[:, None] * freqs[None, :]) % (2 * F) * (math.pi / F) for k in (coarse, fine)]
    return [np.concatenate([np.cos(angle), np.sin(angle)]).astype(np.float32) for angle in angles]


def whiten_kernel(*refs):
    spectra_hbm, gap_hbm, *small_hbm = refs[: 2 + SMALL]
    white_ref, *small_refs = refs[2 + SMALL : 3 + 2 * SMALL]
    spectra_ref, gap_ref, sems = refs[3 + 2 * SMALL :]
    moved = zip((spectra_hbm, gap_hbm, *small_hbm), (spectra_ref, gap_ref, *small_refs))
    copies = [pltpu.make_async_copy(src, dst, sems.at[i]) for i, (src, dst) in enumerate(moved)]
    for copy in copies:
        copy.start()
    for copy in copies[:2]:
        copy.wait()
    stations = spectra_ref.shape[0]
    values = spectra_ref[...].astype(jnp.float32)
    power = jnp.mean(values * values, axis=1, keepdims=True)
    kept = jnp.broadcast_to(SAMPLES - gap_ref[...].astype(jnp.float32), (stations, stations))
    here = lax.broadcasted_iota(jnp.int32, (stations, stations), 0)
    along = lax.broadcasted_iota(jnp.int32, (stations, stations), 1)
    kept = jnp.sum(jnp.where(here == along, kept, 0.0), axis=1, keepdims=True)
    factor = jnp.sqrt(SAMPLES / kept) / jnp.sqrt(power + 1e-06)
    white_ref[...] = (values * factor).astype(jnp.bfloat16) * LIFT
    for copy in copies[2:]:
        copy.wait()


def pick_bins(owner_ref, slot_ref, parity):
    owner = owner_ref[...]
    chip = owner >> 1
    place = jnp.zeros_like(chip)
    for position, number in enumerate(ORDER):
        place = jnp.where(chip == number, position, place)
    local = place * SLOTS_DEV + slot_ref[...]
    return jnp.where((owner & 1) == parity, local, -1)


def into_bins(bins, corr_ref, out_ref):
    pairs = corr_ref.shape[0]
    count = out_ref.shape[0]
    for start in range(0, count, BIN_ROWS):
        ids = lax.broadcasted_iota(jnp.int32, (BIN_ROWS, pairs), 0) + start
        place = (ids == bins).astype(jnp.bfloat16)
        out_ref[start : start + BIN_ROWS, :] = jnp.dot(
            place, corr_ref[...], preferred_element_type=jnp.float32
        ).astype(out_ref.dtype)


def correlate_kernel(
    pairs_ref, owner_ref, slot_ref, white_ref, weight_ref, coarse_ref, fine_ref,
    corr_ref, away_ref, first_ref, second_ref, table_ref,
):
    group = white_ref.shape[0]
    pairs = corr_ref.shape[0]
    ids = lax.broadcasted_iota(jnp.int32, (group, pairs), 0)
    first_ref[...] = (ids == pairs_ref[0:1, :]).astype(jnp.float32).T.astype(jnp.bfloat16)
    second_ref[...] = (ids == pairs_ref[1:2, :]).astype(jnp.float32).T.astype(jnp.bfloat16)
    weight = weight_ref[...] * (0.25 / math.sqrt(F) / (LIFT * LIFT))
    cos_fine, sin_fine = fine_ref[:FINE, :], fine_ref[FINE:, :]
    blocks = LAGS // FINE
    for block in range(blocks):
        cos = weight * coarse_ref[block : block + 1, :]
        sin = weight * coarse_ref[blocks + block : blocks + block + 1, :]
        upper = (cos * cos_fine - sin * sin_fine).astype(jnp.bfloat16)
        lower = (-(sin * cos_fine + cos * sin_fine)).astype(jnp.bfloat16)
        rows = slice(block * FINE, block * FINE + FINE)
        for column in range(0, F, COLUMNS):
            here = slice(column, column + COLUMNS)
            table_ref[rows, 2 * column : 2 * column + COLUMNS] = upper[:, here]
            table_ref[rows, 2 * column + COLUMNS : 2 * column + 2 * COLUMNS] = lower[:, here]

    def pick(one_hot, rows):
        return jnp.dot(one_hot, rows, preferred_element_type=jnp.float32).astype(jnp.bfloat16)

    def lags(cross, table):
        return lax.dot_general(
            cross, table, (((1,), (1,)), ((), ())), preferred_element_type=jnp.float32
        )

    for start in range(0, pairs, ROWS):
        rows = slice(start, start + ROWS)
        one, two = first_ref[rows, :], second_ref[rows, :]
        total = jnp.zeros((ROWS, LAGS), jnp.float32)
        for column in range(0, F, COLUMNS):
            here = slice(column, column + COLUMNS)
            real = white_ref[:, here]
            imag = white_ref[:, F + column : F + column + COLUMNS]
            real_one, imag_one = pick(one, real), pick(one, imag)
            real_two, imag_two = pick(two, real), pick(two, imag)
            cross = jnp.concatenate(
                [
                    (real_one * real_two + imag_one * imag_two).astype(jnp.bfloat16),
                    (imag_one * real_two - real_one * imag_two).astype(jnp.bfloat16),
                ],
                axis=1,
            )
            total += lags(cross, table_ref[:, 2 * column : 2 * column + 2 * COLUMNS])
        corr_ref[rows, :] = total.astype(jnp.bfloat16)
    core = lax.axis_index("seg") & 1
    into_bins(pick_bins(owner_ref, slot_ref, 1 - core), corr_ref, away_ref)


def own_kernel(owner_ref, slot_ref, corr_ref, out_ref):
    core = lax.axis_index("seg") & 1
    into_bins(pick_bins(owner_ref, slot_ref, core), corr_ref, out_ref)


def on_device(spectra, gap_counts, band_weight, pair_list, stack_owner, stack_slot):
    stations = spectra.shape[0]
    pairs = pair_list.shape[0]
    seg = lax.axis_size("seg")
    group = stations * lax.axis_size("grp")
    bins = seg // 2 * SLOTS_DEV
    inputs = (
        spectra, gap_counts.reshape(1, stations), pair_list.T, stack_owner.reshape(1, pairs),
        stack_slot.reshape(1, pairs), band_weight.reshape(1, F), *map(jnp.asarray, tables()),
    )
    white, ends, owner, slot, weight, coarse, fine = pl.pallas_call(
        whiten_kernel,
        in_specs=[pl.BlockSpec(memory_space=pltpu.HBM)] * len(inputs),
        out_shape=[jax.ShapeDtypeStruct(spectra.shape, jnp.bfloat16)]
        + [jax.ShapeDtypeStruct(x.shape, x.dtype) for x in inputs[2:]],
        scratch_shapes=[
            pltpu.VMEM(inputs[0].shape, inputs[0].dtype),
            pltpu.VMEM(inputs[1].shape, inputs[1].dtype),
            pltpu.SemaphoreType.DMA((len(inputs),)),
        ],
        compiler_params=pltpu.CompilerParams(vmem_limit_bytes=8 * MIB),
    )(*[pltpu.with_memory_space_constraint(x, pltpu.HBM) for x in inputs])
    group_rows = lax.all_gather(white.astype(jnp.float16), "grp", axis=0, tiled=True).astype(jnp.bfloat16)

    corr, away = pl.pallas_call(
        correlate_kernel,
        out_shape=[
            jax.ShapeDtypeStruct((pairs, LAGS), jnp.bfloat16),
            jax.ShapeDtypeStruct((bins, LAGS), jnp.bfloat16),
        ],
        scratch_shapes=[
            pltpu.VMEM((pairs, group), jnp.bfloat16),
            pltpu.VMEM((pairs, group), jnp.bfloat16),
            pltpu.VMEM((LAGS, 2 * F), jnp.bfloat16),
        ],
        compiler_params=pltpu.CompilerParams(vmem_limit_bytes=24 * MIB),
    )(
        ends, owner, slot, group_rows, weight, coarse, fine
    )
    arrived = lax.ppermute(away, "seg", [(i, i ^ 1) for i in range(seg)])
    kept = pl.pallas_call(
        own_kernel,
        out_shape=jax.ShapeDtypeStruct((bins, LAGS), jnp.float32),
        compiler_params=pltpu.CompilerParams(vmem_limit_bytes=8 * MIB),
        cost_estimate=pl.CostEstimate(flops=2 * bins * pairs * LAGS, bytes_accessed=2 << 20, transcendentals=0),
    )(owner, slot, corr)
    chip = (kept + arrived.astype(jnp.float32)).astype(jnp.bfloat16).reshape(seg // 2, SLOTS_DEV, LAGS)
    got = lax.all_to_all(
        chip, "seg", split_axis=0, concat_axis=0, tiled=True,
        axis_index_groups=[[2 * chip + core for chip in ORDER] for core in range(2)],
    )
    return jnp.sum(got.astype(jnp.float32), axis=0)


def solution(mesh):
    placed = (
        P(("grp", "seg"), None),
        P(("grp", "seg")),
        P(),
        P(("grp", "seg"), None),
        P(("grp", "seg"), None),
        P(("grp", "seg")),
    )
    return jax.shard_map(
        on_device, mesh=mesh, in_specs=placed, out_specs=P(("grp", "seg"), None), check_vma=False
    )
```
